32 devices in a mesh: fsdp: 8 (over z, y), tp: 4 (over x, core).
Axes of the slice: x: 2, y: 2, z: 4, core: 2. Of those that a mesh axis runs over, the one named last changes fastest.
Arguments:
- tokens: bfloat16 [16384, 768], P(('fsdp', 'tp')), may hold values from -6 to 6
- cotangent: bfloat16 [16384, 768], P(('fsdp', 'tp')), may hold values from -6 to 6
- lengths: int32 [8, 7], P('fsdp'), may hold values from 1 to 512, 2048 in all within a row
- w_query: bfloat16 [2, 768, 768], P(None, 'fsdp', 'tp'), may hold values from -0.21875 to 0.21875
- w_key: bfloat16 [2, 768, 768], P(None, 'fsdp', 'tp'), may hold values from -0.21875 to 0.21875
- w_value: bfloat16 [2, 768, 768], P(None, 'fsdp', 'tp'), may hold values from -0.21875 to 0.21875
- w_out: bfloat16 [2, 768, 768], P(None, 'tp', 'fsdp'), may hold values from -0.625 to 0.625
- w_up: bfloat16 [2, 768, 3072], P(None, 'fsdp', 'tp'), may hold values from -0.21875 to 0.21875
- w_down: bfloat16 [2, 3072, 768], P(None, 'tp', 'fsdp'), may hold values from -0.109375 to 0.109375
- norm_gain: float32 [2, 2, 768], P(None, None, ('fsdp', 'tp')), may hold values from 0.5 to 1.5
- norm_shift: float32 [2, 2, 768], P(None, None, ('fsdp', 'tp')), may hold values from -1.2 to 1.2
- attn_bias: float32 [2, 3, 768], P(None, None, ('fsdp', 'tp')), may hold values from -1.2 to 1.2
- up_bias: float32 [2, 3072], P(None, ('fsdp', 'tp')), may hold values from -1.2 to 1.2
- down_bias: float32 [2, 768], P(None, ('fsdp', 'tp')), may hold values from -1.2 to 1.2
Outputs:
- stream_out: bfloat16 [16384, 768], P(('fsdp', 'tp'))
- grad_tokens: float32 [16384, 768], P(('fsdp', 'tp'))
- grad_query: float32 [2, 768, 768], P(None, 'fsdp', 'tp')
- grad_key: float32 [2, 768, 768], P(None, 'fsdp', 'tp')
- grad_value: float32 [2, 768, 768], P(None, 'fsdp', 'tp')
- grad_out: float32 [2, 768, 768], P(None, 'tp', 'fsdp')
- grad_up: float32 [2, 768, 3072], P(None, 'fsdp', 'tp')
- grad_down: float32 [2, 3072, 768], P(None, 'tp', 'fsdp')
- grad_gain: float32 [2, 2, 768], P(None, None, ('fsdp', 'tp'))
- grad_shift: float32 [2, 2, 768], P(None, None, ('fsdp', 'tp'))
- grad_attn_bias: float32 [2, 3, 768], P(None, None, ('fsdp', 'tp'))
- grad_up_bias: float32 [2, 3072], P(None, ('fsdp', 'tp'))
- grad_down_bias: float32 [2, 768], P(None, ('fsdp', 'tp'))
The draws below stay inside these ranges and needn't reach their ends.
Inputs may be any that keep to these rules, and one draw needn't show every extreme that they name: Each row lists the lengths of the 7 sequences packed in order into one group of 2048 rows; a row sums to 2048 and its largest length is exactly 512.
All inputs are finite; a program needn't handle non-finite values.
Results may differ from the reference program's by a relative error of at most 0.025.
Values may be sent and summed in bfloat16 or wider, within the bound.
No kernel may reach another device: no remote copies, remote signals or barrier semaphores. Data moves between devices by JAX's collectives and lax.ppermute only.
A program may use at most 256 MiB of HBM per device.

```python
import math
import jax
import jax.numpy as jnp
import numpy as np
from jax import lax

D = 768
HEADS = 12
HEAD = 64
FF = 3072
LAYERS = 2
GROUP = 2048
LONGEST = 512
SEQ_GRP = 7
QBLK = 512
TOKENS = 16384
N_FSDP = 8


def block_levels(own_key, extent, cuts, least, top_value):
    gain, own = 1.0, jax.random.fold_in(own_key, 6)
    for axis_at, blocks in cuts:
        steps = jnp.exp(jax.random.uniform(jax.random.fold_in(own, axis_at), (blocks,), jnp.float32, least / len(cuts), top_value / len(cuts)))
        gain = gain * jnp.repeat(steps, extent[axis_at] // blocks).reshape([-1 if axis == axis_at else 1 for axis in range(len(extent))])
    return gain


def length_profile(amount, total, bound, lean):
    weights = [(1 << 20) // math.isqrt(grade ** lean) + 1 for grade in range(2, amount + 1)]
    spare, given = total - bound - (amount - 1), [1] * (amount - 1)
    while spare > 0:
        free = [i for i in range(amount - 1) if given[i] < bound]
        whole, remaining = sum([weights[i] for i in free]), spare
        for i in free:
            addition = min(bound - given[i], max(1, remaining * weights[i] // whole), spare)
            given[i] = given[i] + addition
            spare = spare - addition
    return np.array([bound] + given)


def ragged(stream_key, amount, total, reach, lean):
    if amount == 2:
        one = jax.random.randint(stream_key, (), max(1, total - reach), min(reach, total - 1) + 1)
        return jnp.stack([one, total - one])
    tallies = jnp.asarray(length_profile(amount, total, reach, lean), jnp.int32)
    couples = (amount - 1) // 2
    source_of, receiver = tallies[1:1 + 2 * couples:2], tallies[2:2 + 2 * couples:2]
    room = jnp.minimum(source_of - 1, reach - receiver)
    shifted = jax.random.randint(jax.random.fold_in(stream_key, 1), (couples,), 0, 1 << 20) % (room + 1)
    tallies = tallies.at[1:1 + 2 * couples:2].set(source_of - shifted).at[2:2 + 2 * couples:2].set(receiver + shifted)
    return tallies[jax.random.permutation(jax.random.fold_in(stream_key, 2), amount)]


def noise(own_key, dims, spread, most, shards=(), kind=jnp.bfloat16):
    array = jax.random.normal(own_key, dims, jnp.float32) * spread
    if len(shards) > 0:
        array = block_levels(own_key, dims, shards, -0.22, 0.18) * array
    return jnp.clip(array, min=-most, max=most).astype(kind)


def setup_inputs(seed: int = 0) -> dict:
    key_of = jax.random.split(jax.random.key(seed), 15)
    tokens = noise(key_of[0], (TOKENS, D), 1.0, 6.0, ((0, 32),))
    cotangent = noise(key_of[1], (TOKENS, D), 1.0, 6.0, ((0, 32),))
    lengths = jax.vmap(lambda own: ragged(own, SEQ_GRP, GROUP, LONGEST, 2))(jax.random.split(key_of[2], N_FSDP)).reshape((N_FSDP, SEQ_GRP)).astype(jnp.int32)
    w_query = noise(key_of[3], (LAYERS, D, D), D ** -0.5, 0.21875, ((1, 8), (2, 4)))
    w_key = noise(key_of[4], (LAYERS, D, D), D ** -0.5, 0.21875, ((1, 8), (2, 4)))
    w_value = noise(key_of[5], (LAYERS, D, D), D ** -0.5, 0.21875, ((1, 8), (2, 4)))
    w_out = noise(key_of[6], (LAYERS, D, D), (D // 8) ** -0.5, 0.625, ((1, 4), (2, 8)))
    w_up = noise(key_of[7], (LAYERS, D, FF), D ** -0.5, 0.21875, ((1, 8), (2, 4)))
    w_down = noise(key_of[8], (LAYERS, FF, D), FF ** -0.5, 0.109375, ((1, 4), (2, 8)))
    norm_gain = jnp.clip(1.0 + 0.1 * jax.random.normal(key_of[9], (LAYERS, 2, D), jnp.float32), 0.5, 1.5)
    norm_shift = noise(key_of[10], (LAYERS, 2, D), 0.2, 1.2, ((2, 32),), jnp.float32)
    attn_bias = noise(key_of[11], (LAYERS, 3, D), 0.2, 1.2, ((2, 32),), jnp.float32)
    up_bias = noise(key_of[12], (LAYERS, FF), 0.2, 1.2, ((1, 32),), jnp.float32)
    down_bias = noise(key_of[13], (LAYERS, D), 0.2, 1.2, ((1, 32),), jnp.float32)
    return dict(tokens=tokens, cotangent=cotangent, lengths=lengths, w_query=w_query, w_key=w_key, w_value=w_value, w_out=w_out, w_up=w_up, w_down=w_down, norm_gain=norm_gain, norm_shift=norm_shift, attn_bias=attn_bias, up_bias=up_bias, down_bias=down_bias)


@jax.custom_vjp
def low(v):
    return lax.optimization_barrier(v.astype(jnp.bfloat16)).astype(jnp.float32)

@jax.custom_vjp
def low_back(v):
    return v

def low_keep(v):
    return (low(v), None)

def low_pass(kept, grad):
    return (grad,)

def back_keep(v):
    return (v, None)

def back_low(kept, grad):
    return (low(grad),)
low.defvjp(low_keep, low_pass)
low_back.defvjp(back_keep, back_low)
eps = 1e-05
masked_fill = -1e+30
precise = lax.Precision.HIGHEST

def layer_norm(values, gain_row, shift_row):
    row_mean = lax.optimization_barrier(jnp.mean(values, axis=-1, keepdims=True))
    centred = values - row_mean
    row_var = lax.optimization_barrier(jnp.mean(centred * centred, axis=-1, keepdims=True))
    return centred * lax.rsqrt(row_var + eps) * gain_row + shift_row

def matmul(left, right):
    return jnp.dot(left, right, precision=precise)

def segment_ids(group_lengths):
    seq_ends = jnp.cumsum(group_lengths)
    row_ids = jnp.arange(GROUP, dtype=jnp.int32)
    return lax.optimization_barrier(jnp.sum((row_ids[:, None] >= seq_ends[None, :]).astype(jnp.int32), axis=1))

def attend_group(packed):
    queries, key_rows, value_rows, segments = packed
    row_ids = jnp.arange(GROUP, dtype=jnp.int32)

    def attend_block(first_row):
        query_block = lax.dynamic_slice_in_dim(queries, first_row, QBLK, 0)
        query_seg = lax.dynamic_slice_in_dim(segments, first_row, QBLK, 0)
        query_pos = first_row + jnp.arange(QBLK, dtype=jnp.int32)
        raw_scores = low_back(jnp.einsum('qhd,khd->hqk', query_block, key_rows, precision=precise))
        scores = raw_scores * HEAD ** (-0.5)
        allowed = (query_seg[:, None] == segments[None, :]) & (row_ids[None, :] <= query_pos[:, None])
        scores = jnp.where(allowed[None], scores, masked_fill)
        attn_prob = low(jax.nn.softmax(scores, axis=-1))
        return jnp.einsum('hqk,khd->qhd', attn_prob, value_rows, precision=precise)
    starts = jnp.arange(GROUP // QBLK, dtype=jnp.int32) * QBLK
    blocks = lax.map(jax.checkpoint(attend_block), starts)
    return blocks.reshape(GROUP, HEADS, HEAD)

def reference(tokens, cotangent, lengths, w_query, w_key, w_value, w_out, w_up, w_down, norm_gain, norm_shift, attn_bias, up_bias, down_bias):
    params = (w_query.astype(jnp.float32), w_key.astype(jnp.float32), w_value.astype(jnp.float32), w_out.astype(jnp.float32), w_up.astype(jnp.float32), w_down.astype(jnp.float32), norm_gain.astype(jnp.float32), norm_shift.astype(jnp.float32), attn_bias.astype(jnp.float32), up_bias.astype(jnp.float32), down_bias.astype(jnp.float32))
    segments = jax.vmap(segment_ids)(lengths)

    def shaped(matrix):
        return matrix.reshape(N_FSDP, GROUP, HEADS, HEAD)

    def forward_pass(stream, weights):
        wt_query, wt_key, wt_value, wt_out, wt_up, wt_down, gains, shifts, biases, bias_hidden, bias_down = weights
        for layer_index in range(LAYERS):
            normed = low(layer_norm(stream, gains[layer_index, 0], shifts[layer_index, 0]))
            queries = low(low_back(matmul(normed, wt_query[layer_index]) + biases[layer_index, 0]))
            key_rows = low(low_back(matmul(normed, wt_key[layer_index])))
            value_rows = low(low_back(matmul(normed, wt_value[layer_index]) + biases[layer_index, 1]))
            attended = lax.map(attend_group, (shaped(queries), shaped(key_rows), shaped(value_rows), segments))
            attended = low(low_back(attended.reshape(TOKENS, D)))
            stream = stream + low_back(matmul(attended, wt_out[layer_index])) + biases[layer_index, 2]
            normed = low(layer_norm(stream, gains[layer_index, 1], shifts[layer_index, 1]))
            hidden = low(jax.nn.gelu(low_back(matmul(normed, wt_up[layer_index]) + bias_hidden[layer_index])))
            stream = stream + low_back(matmul(hidden, wt_down[layer_index])) + bias_down[layer_index]
        return stream
    result, pullback = jax.vjp(forward_pass, tokens.astype(jnp.float32), params)
    grad_stream, grad_params = pullback(cotangent.astype(jnp.float32))
    return (result.astype(jnp.bfloat16), grad_stream, grad_params[0], grad_params[1], grad_params[2], grad_params[3], grad_params[4], grad_params[5], grad_params[6], grad_params[7], grad_params[8], grad_params[9], grad_params[10])
```

```python
import functools

import jax
import jax.numpy as jnp
from jax import lax
from jax.experimental import pallas as pl
from jax.experimental.pallas import tpu as pltpu
from jax.sharding import PartitionSpec as P

HEAD = 64
LANES = 128
QROWS = 256
eps = 1e-05
masked_fill = -1e30
VMEM_BYTES = 56 * 1024 * 1024
BOTH = ("fsdp", "tp")

f32 = jnp.float32
bf16 = jnp.bfloat16


def dot_nn(left, right):
    return lax.dot_general(left, right, (((1,), (0,)), ((), ())), preferred_element_type=f32)


def dot_nt(left, right):
    return lax.dot_general(left, right, (((1,), (1,)), ((), ())), preferred_element_type=f32)


def dot_tn(left, right):
    return lax.dot_general(left, right, (((0,), (0,)), ((), ())), preferred_element_type=f32)


def fill_bias(seg_q_ref, seg_k_ref, bias_ref, rows):
    window = rows + QROWS
    for first in range(0, rows, QROWS):
        row_pos = rows + first + lax.broadcasted_iota(jnp.int32, (QROWS, window), 0)
        col_pos = first + lax.broadcasted_iota(jnp.int32, (QROWS, window), 1)
        same = seg_q_ref[first : first + QROWS, :] == seg_k_ref[:, first : first + window]
        bias_ref[first : first + QROWS, :] = jnp.where(same & (col_pos <= row_pos), 0.0, masked_fill)


def attend_forward_body(rows, seg_q_ref, seg_k_ref, q_ref, k_ref, v_ref, o_ref, lse_ref, bias_ref):
    window = rows + QROWS

    @pl.when(pl.program_id(0) == 0)
    def _():
        fill_bias(seg_q_ref, seg_k_ref, bias_ref, rows)

    low_lane = lax.broadcasted_iota(jnp.int32, (QROWS, LANES), 1) < HEAD
    for first in range(0, rows, QROWS):
        here = slice(first, first + QROWS)
        keys = k_ref[first : first + window, :]
        values = v_ref[first : first + window, :]
        bias = bias_ref[here, :]
        queries = q_ref[here, :] * jnp.asarray(HEAD**-0.5, bf16)
        outs, lses = [], []
        for head in range(2):
            mine = low_lane if head == 0 else ~low_lane
            scores = dot_nt(jnp.where(mine, queries, 0), keys) + bias
            top = jnp.max(scores, axis=-1, keepdims=True)
            terms = jnp.exp(scores - top)
            total = jnp.sum(terms, axis=-1, keepdims=True)
            outs.append(dot_nn(terms.astype(bf16), values) * (1.0 / total))
            lses.append(top + jnp.log(total))
        o_ref[here, :] = jnp.where(low_lane, outs[0], outs[1]).astype(bf16)
        lse_ref[here, :] = jnp.where(low_lane, lses[0], lses[1])


def attend_backward_body(
    rows, seg_q_ref, seg_k_ref, q_ref, k_ref, v_ref, o_ref, lse_ref, do_ref,
    dq_ref, dk_ref, dv_ref, bias_ref, dk_acc, dv_acc,
):
    window = rows + QROWS

    @pl.when(pl.program_id(0) == 0)
    def _():
        fill_bias(seg_q_ref, seg_k_ref, bias_ref, rows)

    dk_acc[...] = jnp.zeros_like(dk_acc)
    dv_acc[...] = jnp.zeros_like(dv_acc)
    low_lane = lax.broadcasted_iota(jnp.int32, (QROWS, LANES), 1) < HEAD
    for first in range(0, rows, QROWS):
        here = slice(first, first + QROWS)
        span = slice(first, first + window)
        keys = k_ref[span, :]
        values = v_ref[span, :]
        bias = bias_ref[here, :]
        queries = q_ref[here, :] * jnp.asarray(HEAD**-0.5, bf16)
        grads = do_ref[here, :]
        product = grads.astype(f32) * o_ref[here, :].astype(f32)
        lse_both = lse_ref[here, :]
        dqs, dks, dvs = [], [], []
        for head in range(2):
            mine = low_lane if head == 0 else ~low_lane
            my_queries = jnp.where(mine, queries, 0)
            my_grads = jnp.where(mine, grads, 0)
            inner = jnp.sum(jnp.where(mine, product, 0.0), axis=-1, keepdims=True)
            lse = lse_both[:, head * HEAD : head * HEAD + 1]
            probs = jnp.exp(dot_nt(my_queries, keys) + bias - lse)
            draw = (probs * (dot_nt(my_grads, values) - inner)).astype(bf16)
            dvs.append(dot_tn(probs.astype(bf16), my_grads))
            dks.append(dot_tn(draw, my_queries))
            dqs.append(dot_nn(draw, keys))
        dv_acc[span, :] += dvs[0] + dvs[1]
        dk_acc[span, :] += dks[0] + dks[1]
        dq_ref[here, :] = (jnp.where(low_lane, dqs[0], dqs[1]) * HEAD**-0.5).astype(bf16)
    dk_ref[...] = dk_acc[...].astype(bf16)
    dv_ref[...] = dv_acc[...].astype(bf16)


def pair_spec(rows):
    return pl.BlockSpec((rows, LANES), lambda pair: (0, pair))


def whole_spec(shape):
    return pl.BlockSpec(shape, lambda *_: (0,) * len(shape))


def attend_forward(seg_q, seg_k, queries, keys, values):
    rows, width = queries.shape
    return pl.pallas_call(
        functools.partial(attend_forward_body, rows),
        grid=(width // LANES,),
        in_specs=[
            whole_spec(seg_q.shape), whole_spec(seg_k.shape),
            pair_spec(rows), pair_spec(2 * rows), pair_spec(2 * rows),
        ],
        out_specs=[pair_spec(rows), pair_spec(rows)],
        out_shape=[
            jax.ShapeDtypeStruct((rows, width), bf16),
            jax.ShapeDtypeStruct((rows, width), f32),
        ],
        scratch_shapes=[pltpu.VMEM((rows, rows + QROWS), f32)],
        compiler_params=pltpu.CompilerParams(vmem_limit_bytes=VMEM_BYTES),
        cost_estimate=pl.CostEstimate(
            flops=16 * rows * (rows + QROWS) * width, bytes_accessed=6 * rows * width * 2,
            transcendentals=rows * rows * width // HEAD,
        ),
        name="attend_forward",
    )(seg_q, seg_k, queries, keys, values)


def attend_backward(seg_q, seg_k, queries, keys, values, attended, lse, grad_attended):
    rows, width = queries.shape
    return pl.pallas_call(
        functools.partial(attend_backward_body, rows),
        grid=(width // LANES,),
        in_specs=[
            whole_spec(seg_q.shape), whole_spec(seg_k.shape),
            pair_spec(rows), pair_spec(2 * rows), pair_spec(2 * rows),
            pair_spec(rows), pair_spec(rows), pair_spec(rows),
        ],
        out_specs=[pair_spec(rows), pair_spec(2 * rows), pair_spec(2 * rows)],
        out_shape=[
            jax.ShapeDtypeStruct((rows, width), bf16),
            jax.ShapeDtypeStruct((2 * rows, width), bf16),
            jax.ShapeDtypeStruct((2 * rows, width), bf16),
        ],
        scratch_shapes=[
            pltpu.VMEM((rows, rows + QROWS), f32),
            pltpu.VMEM((2 * rows, LANES), f32),
            pltpu.VMEM((2 * rows, LANES), f32),
        ],
        compiler_params=pltpu.CompilerParams(vmem_limit_bytes=VMEM_BYTES),
        cost_estimate=pl.CostEstimate(
            flops=40 * rows * (rows + QROWS) * width, bytes_accessed=12 * rows * width * 2,
            transcendentals=rows * rows * width // HEAD,
        ),
        name="attend_backward",
    )(seg_q, seg_k, queries, keys, values, attended, lse, grad_attended)


GELU_A = 0.7978845608028654
GELU_B = 0.044715


def gelu_parts(pre):
    square = pre * pre
    bend = jnp.tanh(GELU_A * pre * (1.0 + GELU_B * square))
    half = 0.5 * (1.0 + bend)
    slope = half + 0.5 * pre * (1.0 - bend * bend) * (GELU_A * (1.0 + 3.0 * GELU_B * square))
    return pre * half, slope


def feed_forward_body(n_ref, up_ref, down_ref, bias_ref, pre_ref, out_ref):
    @pl.when(pl.program_id(0) == 0)
    def _():
        out_ref[...] = jnp.zeros_like(out_ref)

    pre = dot_nn(n_ref[...], up_ref[0]) + bias_ref[0]
    pre_ref[0] = pre
    hidden = gelu_parts(pre)[0].astype(bf16)
    out_ref[...] += dot_nt(hidden, down_ref[0])


def feed_forward(normed, up, down, bias):
    rows, width = normed.shape
    parts, _, cols = up.shape
    part = pl.BlockSpec((1, width, cols), lambda t: (t, 0, 0))
    return pl.pallas_call(
        feed_forward_body,
        grid=(parts,),
        in_specs=[
            whole_spec((rows, width)), part, part,
            pl.BlockSpec((1, 1, cols), lambda t: (t, 0, 0)),
        ],
        out_specs=[pl.BlockSpec((1, rows, cols), lambda t: (t, 0, 0)), whole_spec((rows, width))],
        out_shape=[
            jax.ShapeDtypeStruct((parts, rows, cols), f32),
            jax.ShapeDtypeStruct((rows, width), f32),
        ],
        compiler_params=pltpu.CompilerParams(vmem_limit_bytes=VMEM_BYTES),
        cost_estimate=pl.CostEstimate(
            flops=4 * rows * width * cols * parts, bytes_accessed=4 * parts * width * cols + 4 * parts * rows * cols,
            transcendentals=rows * cols * parts,
        ),
        name="feed_forward",
    )(normed, up, down, bias)


def feed_backward_body(
    g_ref, gt_ref, nt_ref, pre_ref, up_ref, down_ref, gup_ref, gdown_ref, gbias_ref, dn_ref
):
    @pl.when(pl.program_id(0) == 0)
    def _():
        dn_ref[...] = jnp.zeros_like(dn_ref)

    hidden, slope = gelu_parts(pre_ref[0])
    gdown_ref[0] = dot_nn(gt_ref[...], hidden.astype(bf16)).astype(bf16)
    dpre = (dot_nn(g_ref[...], down_ref[0]) * slope).astype(bf16)
    gbias_ref[0] = jnp.sum(dpre.astype(f32), axis=0, keepdims=True)
    gup_ref[0] = dot_nn(nt_ref[...], dpre).astype(bf16)
    dn_ref[...] += dot_nt(dpre, up_ref[0])


def feed_backward(grad_low, normed, pre, up, down):
    rows, width = normed.shape
    parts, _, cols = up.shape
    part = pl.BlockSpec((1, width, cols), lambda t: (t, 0, 0))
    return pl.pallas_call(
        feed_backward_body,
        grid=(parts,),
        in_specs=[
            whole_spec((rows, width)), whole_spec((width, rows)), whole_spec((width, rows)),
            pl.BlockSpec((1, rows, cols), lambda t: (t, 0, 0)), part, part,
        ],
        out_specs=[
            part, part, pl.BlockSpec((1, 1, cols), lambda t: (t, 0, 0)), whole_spec((rows, width)),
        ],
        out_shape=[
            jax.ShapeDtypeStruct((parts, width, cols), bf16),
            jax.ShapeDtypeStruct((parts, width, cols), bf16),
            jax.ShapeDtypeStruct((parts, 1, cols), f32),
            jax.ShapeDtypeStruct((rows, width), f32),
        ],
        compiler_params=pltpu.CompilerParams(vmem_limit_bytes=VMEM_BYTES),
        cost_estimate=pl.CostEstimate(
            flops=8 * rows * width * cols * parts, bytes_accessed=8 * parts * width * cols + 4 * parts * rows * cols,
            transcendentals=rows * cols * parts,
        ),
        name="feed_backward",
    )(grad_low, grad_low.T, normed.T, pre, up, down)


def norm_stats(values):
    mean = jnp.mean(values, axis=-1, keepdims=True)
    centred = values - mean
    var = jnp.mean(centred * centred, axis=-1, keepdims=True)
    scale = lax.rsqrt(var + eps)
    return centred * scale, scale


def norm_forward(values, gain, shift):
    return (norm_stats(values)[0] * gain + shift).astype(bf16)


def norm_backward(values, gain, grad):
    unit, scale = norm_stats(values)
    inner = grad * gain
    back = scale * (
        inner
        - jnp.mean(inner, axis=-1, keepdims=True)
        - unit * jnp.mean(inner * unit, axis=-1, keepdims=True)
    )
    return back, jnp.sum(grad * unit, axis=0), jnp.sum(grad, axis=0)


def gather_weights(shard):
    fsdp, tp = lax.axis_size("fsdp"), lax.axis_size("tp")
    rows, cols = shard.shape
    whole = lax.all_gather(shard, BOTH, axis=0, tiled=False).reshape(fsdp, tp, rows, cols)
    return whole.transpose(1, 0, 2, 3).reshape(tp, fsdp * rows, cols)


def scatter_grads(grad):
    fsdp, tp = lax.axis_size("fsdp"), lax.axis_size("tp")
    rows, cols = grad.shape[1] // fsdp, grad.shape[2]
    parts = grad.reshape(tp, fsdp, rows, cols).transpose(1, 0, 2, 3).reshape(-1, cols)
    return lax.psum_scatter(parts, BOTH, scatter_dimension=0, tiled=True).astype(f32)


def from_previous(rows):
    tp = lax.axis_size("tp")
    return lax.ppermute(rows, "tp", [(i, i + 1) for i in range(tp - 1)])


def to_previous(rows):
    tp = lax.axis_size("tp")
    return lax.ppermute(rows, "tp", [(i + 1, i) for i in range(tp - 1)])


def side_by_side(parts):
    return jnp.concatenate([parts[t] for t in range(parts.shape[0])], axis=1)


def apart(whole, parts):
    cols = whole.shape[1] // parts
    return [whole[:, t * cols : (t + 1) * cols] for t in range(parts)]


def on_device(
    tokens, cotangent, lengths, w_query, w_key, w_value, w_out, w_up, w_down,
    norm_gain, norm_shift, attn_bias, up_bias, down_bias,
):
    fsdp, tp = lax.axis_size("fsdp"), lax.axis_size("tp")
    devices = fsdp * tp
    tp_index = lax.axis_index("tp")
    rows, width = tokens.shape
    layers = w_query.shape[0]
    head_cols, hidden_cols = w_query.shape[2], w_up.shape[2]

    smalls = [norm_gain, norm_shift, attn_bias, up_bias, down_bias]
    packed = jnp.concatenate([part.reshape(1, -1) for part in smalls], axis=1)
    packed_all = lax.all_gather(packed, BOTH, axis=0, tiled=True)
    wholes, at = [], 0
    for part in smalls:
        size, lead, last = part.size, part.shape[:-1], part.shape[-1]
        piece = packed_all[:, at : at + size].reshape((devices,) + part.shape)
        wholes.append(jnp.moveaxis(piece, 0, -2).reshape(lead + (devices * last,)))
        at += size
    gain_all, shift_all, bias_attn, bias_up, bias_down = wholes

    weights = []
    for layer in range(layers):
        attn_shard = jnp.concatenate(
            [w_query[layer], w_key[layer], w_value[layer], w_out[layer].T], axis=1
        )
        weights.append(
            (gather_weights(attn_shard), gather_weights(w_up[layer]), gather_weights(w_down[layer].T))
        )

    seq_ends = jnp.cumsum(lengths[0])
    first_row = tp_index * rows
    key_ids = first_row - rows + jnp.arange(2 * rows, dtype=jnp.int32)
    segments = jnp.sum((key_ids[:, None] >= seq_ends[None, :]).astype(jnp.int32), axis=1)
    segments = jnp.where(key_ids >= 0, segments, -1)
    seg_q, seg_k = segments[rows:, None], segments[None, :]

    stream = tokens.astype(f32)
    saved = []
    for layer in range(layers):
        attn_w, up, down = weights[layer]
        wq, wk, wv, wo = (
            side_by_side(attn_w[:, :, n * head_cols : (n + 1) * head_cols]) for n in range(4)
        )
        normed = norm_forward(stream, gain_all[layer, 0], shift_all[layer, 0])
        wide = jnp.concatenate([from_previous(normed), normed], axis=0)
        queries = (dot_nn(normed, wq) + bias_attn[layer, 0]).astype(bf16)
        keys = dot_nn(wide, wk).astype(bf16)
        values = (dot_nn(wide, wv) + bias_attn[layer, 1]).astype(bf16)
        attended, lse = attend_forward(seg_q, seg_k, queries, keys, values)
        mid = stream + dot_nt(attended, wo) + bias_attn[layer, 2]
        normed_mid = norm_forward(mid, gain_all[layer, 1], shift_all[layer, 1])
        pre, fed = feed_forward(
            normed_mid, up, down, bias_up[layer].reshape(tp, 1, hidden_cols)
        )
        saved.append(
            (stream, wide, queries, keys, values, attended, lse, mid, normed_mid, pre, wq, wk, wv, wo)
        )
        stream = mid + fed + bias_down[layer]

    grad = cotangent.astype(f32)
    shards = [None] * layers
    small_grads = [None] * layers
    for layer in reversed(range(layers)):
        _, up, down = weights[layer]
        stream_in, wide, queries, keys, values, attended, lse, mid, normed_mid, pre, wq, wk, wv, wo = (
            saved[layer]
        )
        normed = wide[rows:]
        grad_bias_down = jnp.sum(grad, axis=0)
        grad_low = grad.astype(bf16)
        grad_up, grad_down, grad_bias_up, dn = feed_backward(grad_low, normed_mid, pre, up, down)
        up_shard, down_shard = scatter_grads(grad_up), scatter_grads(grad_down)
        back, gain_second, shift_second = norm_backward(mid, gain_all[layer, 1], dn)
        grad = grad + back
        grad_bias_out = jnp.sum(grad, axis=0)
        grad_low = grad.astype(bf16)
        grad_wo = dot_tn(grad_low, attended).astype(bf16)
        grad_attended = dot_nn(grad_low, wo).astype(bf16)
        dq, dk, dv = attend_backward(seg_q, seg_k, queries, keys, values, attended, lse, grad_attended)
        dn_wide = dot_nt(dk, wk) + dot_nt(dv, wv)
        dn_before = to_previous(dn_wide[:rows].astype(bf16)).astype(f32)
        grad_wq = dot_tn(normed, dq).astype(bf16)
        grad_wk = dot_tn(wide, dk).astype(bf16)
        grad_wv = dot_tn(wide, dv).astype(bf16)
        grad_attn = jnp.stack(
            [
                jnp.concatenate(four, axis=1)
                for four in zip(*(apart(whole, tp) for whole in (grad_wq, grad_wk, grad_wv, grad_wo)))
            ]
        )
        attn_shard = scatter_grads(grad_attn)
        dn = dn_wide[rows:] + dot_nt(dq, wq) + dn_before
        back, gain_first, shift_first = norm_backward(stream_in, gain_all[layer, 0], dn)
        grad = grad + back
        shards[layer] = tuple(attn_shard[:, n * head_cols : (n + 1) * head_cols] for n in range(3)) + (
            attn_shard[:, 3 * head_cols :].T, up_shard, down_shard.T,
        )
        small_grads[layer] = (
            jnp.stack([gain_first, gain_second]),
            jnp.stack([shift_first, shift_second]),
            jnp.stack(
                [jnp.sum(dq.astype(f32), axis=0), jnp.sum(dv.astype(f32), axis=0), grad_bias_out]
            ),
            grad_bias_up.reshape(-1),
            grad_bias_down,
        )

    pieces = []
    for member, part in enumerate(smalls):
        whole = jnp.stack([small_grads[layer][member] for layer in range(layers)])
        last = part.shape[-1]
        split = whole.reshape(part.shape[:-1] + (devices, last))
        pieces.append(jnp.moveaxis(split, -2, 0).reshape(devices, part.size))
    summed = lax.psum_scatter(
        jnp.concatenate(pieces, axis=1), BOTH, scatter_dimension=0, tiled=True
    )
    small_outs, at = [], 0
    for part in smalls:
        small_outs.append(summed[:, at : at + part.size].reshape(part.shape))
        at += part.size
    stacked = [jnp.stack([shards[layer][n] for layer in range(layers)]) for n in range(6)]
    return (stream.astype(bf16), grad, *stacked, *small_outs)


def solution(mesh):
    tokens_spec = P(BOTH, None)
    in_spec, out_spec = P(None, "fsdp", "tp"), P(None, "tp", "fsdp")
    matrices = (in_spec, in_spec, in_spec, out_spec, in_spec, out_spec)
    smalls = (P(None, None, BOTH),) * 3 + (P(None, BOTH),) * 2
    return jax.shard_map(
        on_device,
        mesh=mesh,
        in_specs=(tokens_spec, tokens_spec, P("fsdp", None)) + matrices + smalls,
        out_specs=(tokens_spec, tokens_spec) + matrices + smalls,
        check_vma=False,
    )
```

```python
import functools

import jax
import jax.numpy as jnp
from jax import lax
from jax.experimental import pallas as pl
from jax.experimental.pallas import tpu as pltpu
from jax.sharding import PartitionSpec as P

HEAD = 64
LANES = 128
QROWS = 256
eps = 1e-05
masked_fill = -1e30
VMEM_BYTES = 56 * 1024 * 1024
BOTH = ("fsdp", "tp")

f32 = jnp.float32
bf16 = jnp.bfloat16


def dot_nn(left, right):
    return lax.dot_general(left, right, (((1,), (0,)), ((), ())), preferred_element_type=f32)


def dot_nt(left, right):
    return lax.dot_general(left, right, (((1,), (1,)), ((), ())), preferred_element_type=f32)


def dot_tn(left, right):
    return lax.dot_general(left, right, (((0,), (0,)), ((), ())), preferred_element_type=f32)


def tie(value, deps):
    deps = list(deps)
    return pl.pallas_call(
        lambda *refs: None,
        in_specs=[pl.BlockSpec(memory_space=pl.ANY)] * (1 + len(deps)),
        out_specs=pl.BlockSpec(memory_space=pl.ANY),
        out_shape=jax.ShapeDtypeStruct(value.shape, value.dtype),
        input_output_aliases={0: 0},
        name="tie",
    )(value, *deps)


def dep_specs(deps):
    return [pl.BlockSpec(memory_space=pl.ANY)] * len(deps)


def skip_deps(body, inputs, count):
    return lambda *refs: body(*refs[:inputs], *refs[inputs + count :])


COST = pl.CostEstimate(flops=1000, bytes_accessed=1000, transcendentals=0)


def fill_bias(seg_q_ref, seg_k_ref, bias_ref, rows):
    window = rows + QROWS
    for first in range(0, rows, QROWS):
        row_pos = rows + first + lax.broadcasted_iota(jnp.int32, (QROWS, window), 0)
        col_pos = first + lax.broadcasted_iota(jnp.int32, (QROWS, window), 1)
        same = seg_q_ref[first : first + QROWS, :] == seg_k_ref[:, first : first + window]
        bias_ref[first : first + QROWS, :] = jnp.where(same & (col_pos <= row_pos), 0.0, masked_fill)


def attend_forward_body(rows, seg_q_ref, seg_k_ref, q_ref, k_ref, v_ref, o_ref, lse_ref, bias_ref):
    window = rows + QROWS

    @pl.when(pl.program_id(0) == 0)
    def _():
        fill_bias(seg_q_ref, seg_k_ref, bias_ref, rows)

    low_lane = lax.broadcasted_iota(jnp.int32, (QROWS, LANES), 1) < HEAD
    for first in range(0, rows, QROWS):
        here = slice(first, first + QROWS)
        keys = k_ref[first : first + window, :]
        values = v_ref[first : first + window, :]
        bias = bias_ref[here, :]
        queries = q_ref[here, :] * jnp.asarray(HEAD**-0.5, bf16)
        outs, lses = [], []
        for head in range(2):
            mine = low_lane if head == 0 else ~low_lane
            scores = dot_nt(jnp.where(mine, queries, 0), keys) + bias
            top = jnp.max(scores, axis=-1, keepdims=True)
            terms = jnp.exp(scores - top)
            total = jnp.sum(terms, axis=-1, keepdims=True)
            outs.append(dot_nn(terms.astype(bf16), values) * (1.0 / total))
            lses.append(top + jnp.log(total))
        o_ref[here, :] = jnp.where(low_lane, outs[0], outs[1]).astype(bf16)
        lse_ref[here, :] = jnp.where(low_lane, lses[0], lses[1])


def attend_backward_body(
    rows, seg_q_ref, seg_k_ref, q_ref, k_ref, v_ref, o_ref, lse_ref, do_ref,
    dq_ref, dk_ref, dv_ref, bias_ref, dk_acc, dv_acc,
):
    window = rows + QROWS

    @pl.when(pl.program_id(0) == 0)
    def _():
        fill_bias(seg_q_ref, seg_k_ref, bias_ref, rows)

    dk_acc[...] = jnp.zeros_like(dk_acc)
    dv_acc[...] = jnp.zeros_like(dv_acc)
    low_lane = lax.broadcasted_iota(jnp.int32, (QROWS, LANES), 1) < HEAD
    for first in range(0, rows, QROWS):
        here = slice(first, first + QROWS)
        span = slice(first, first + window)
        keys = k_ref[span, :]
        values = v_ref[span, :]
        bias = bias_ref[here, :]
        queries = q_ref[here, :] * jnp.asarray(HEAD**-0.5, bf16)
        grads = do_ref[here, :]
        product = grads.astype(f32) * o_ref[here, :].astype(f32)
        lse_both = lse_ref[here, :]
        dqs, dks, dvs = [], [], []
        for head in range(2):
            mine = low_lane if head == 0 else ~low_lane
            my_queries = jnp.where(mine, queries, 0)
            my_grads = jnp.where(mine, grads, 0)
            inner = jnp.sum(jnp.where(mine, product, 0.0), axis=-1, keepdims=True)
            lse = lse_both[:, head * HEAD : head * HEAD + 1]
            probs = jnp.exp(dot_nt(my_queries, keys) + bias - lse)
            draw = (probs * (dot_nt(my_grads, values) - inner)).astype(bf16)
            dvs.append(dot_tn(probs.astype(bf16), my_grads))
            dks.append(dot_tn(draw, my_queries))
            dqs.append(dot_nn(draw, keys))
        dv_acc[span, :] += dvs[0] + dvs[1]
        dk_acc[span, :] += dks[0] + dks[1]
        dq_ref[here, :] = (jnp.where(low_lane, dqs[0], dqs[1]) * HEAD**-0.5).astype(bf16)
    dk_ref[...] = dk_acc[...].astype(bf16)
    dv_ref[...] = dv_acc[...].astype(bf16)


def pair_spec(rows):
    return pl.BlockSpec((rows, LANES), lambda pair: (0, pair))


def whole_spec(shape):
    return pl.BlockSpec(shape, lambda *_: (0,) * len(shape))


def attend_forward(seg_q, seg_k, queries, keys, values, deps):
    rows, width = queries.shape
    return pl.pallas_call(
        skip_deps(functools.partial(attend_forward_body, rows), 5, len(deps)),
        grid=(width // LANES,),
        in_specs=[
            whole_spec(seg_q.shape), whole_spec(seg_k.shape),
            pair_spec(rows), pair_spec(2 * rows), pair_spec(2 * rows),
        ] + dep_specs(deps),
        out_specs=[pair_spec(rows), pair_spec(rows)],
        out_shape=[
            jax.ShapeDtypeStruct((rows, width), bf16),
            jax.ShapeDtypeStruct((rows, width), f32),
        ],
        scratch_shapes=[pltpu.VMEM((rows, rows + QROWS), f32)],
        compiler_params=pltpu.CompilerParams(vmem_limit_bytes=VMEM_BYTES),
        cost_estimate=COST,
        name="attend_forward",
    )(seg_q, seg_k, queries, keys, values, *deps)


def attend_backward(seg_q, seg_k, queries, keys, values, attended, lse, grad_attended, deps):
    rows, width = queries.shape
    return pl.pallas_call(
        skip_deps(functools.partial(attend_backward_body, rows), 8, len(deps)),
        grid=(width // LANES,),
        in_specs=[
            whole_spec(seg_q.shape), whole_spec(seg_k.shape),
            pair_spec(rows), pair_spec(2 * rows), pair_spec(2 * rows),
            pair_spec(rows), pair_spec(rows), pair_spec(rows),
        ] + dep_specs(deps),
        out_specs=[pair_spec(rows), pair_spec(2 * rows), pair_spec(2 * rows)],
        out_shape=[
            jax.ShapeDtypeStruct((rows, width), bf16),
            jax.ShapeDtypeStruct((2 * rows, width), bf16),
            jax.ShapeDtypeStruct((2 * rows, width), bf16),
        ],
        scratch_shapes=[
            pltpu.VMEM((rows, rows + QROWS), f32),
            pltpu.VMEM((2 * rows, LANES), f32),
            pltpu.VMEM((2 * rows, LANES), f32),
        ],
        compiler_params=pltpu.CompilerParams(vmem_limit_bytes=VMEM_BYTES),
        cost_estimate=COST,
        name="attend_backward",
    )(seg_q, seg_k, queries, keys, values, attended, lse, grad_attended, *deps)


GELU_A = 0.7978845608028654
GELU_B = 0.044715


def gelu_parts(pre):
    square = pre * pre
    bend = jnp.tanh(GELU_A * pre * (1.0 + GELU_B * square))
    half = 0.5 * (1.0 + bend)
    slope = half + 0.5 * pre * (1.0 - bend * bend) * (GELU_A * (1.0 + 3.0 * GELU_B * square))
    return pre * half, slope


def feed_forward_body(n_ref, up_ref, down_ref, bias_ref, pre_ref, out_ref):
    @pl.when(pl.program_id(0) == 0)
    def _():
        out_ref[...] = jnp.zeros_like(out_ref)

    pre = dot_nn(n_ref[...], up_ref[0]) + bias_ref[0]
    pre_ref[0] = pre
    hidden = gelu_parts(pre)[0].astype(bf16)
    out_ref[...] += dot_nt(hidden, down_ref[0])


def feed_forward(normed, updown, bias, deps):
    rows, width = normed.shape
    parts, _, cols = updown.shape
    cols = cols // 2
    up_part = pl.BlockSpec((1, width, cols), lambda t: (t, 0, 0))
    down_part = pl.BlockSpec((1, width, cols), lambda t: (t, 0, 1))
    return pl.pallas_call(
        skip_deps(feed_forward_body, 4, len(deps)),
        grid=(parts,),
        in_specs=[
            whole_spec((rows, width)), up_part, down_part,
            pl.BlockSpec((1, 1, cols), lambda t: (t, 0, 0)),
        ] + dep_specs(deps),
        out_specs=[pl.BlockSpec((1, rows, cols), lambda t: (t, 0, 0)), whole_spec((rows, width))],
        out_shape=[
            jax.ShapeDtypeStruct((parts, rows, cols), f32),
            jax.ShapeDtypeStruct((rows, width), f32),
        ],
        compiler_params=pltpu.CompilerParams(vmem_limit_bytes=VMEM_BYTES),
        cost_estimate=COST,
        name="feed_forward",
    )(normed, updown, updown, bias, *deps)


def feed_backward_body(
    g_ref, gt_ref, nt_ref, pre_ref, up_ref, down_ref, gupdown_ref, gbias_ref, dn_ref
):
    @pl.when(pl.program_id(0) == 0)
    def _():
        dn_ref[...] = jnp.zeros_like(dn_ref)

    hidden, slope = gelu_parts(pre_ref[0])
    cols = hidden.shape[1]
    gupdown_ref[0, :, cols:] = dot_nn(gt_ref[...], hidden.astype(bf16)).astype(bf16)
    dpre = (dot_nn(g_ref[...], down_ref[0]) * slope).astype(bf16)
    gbias_ref[0] = jnp.sum(dpre.astype(f32), axis=0, keepdims=True)
    gupdown_ref[0, :, :cols] = dot_nn(nt_ref[...], dpre).astype(bf16)
    dn_ref[...] += dot_nt(dpre, up_ref[0])


def feed_backward(grad_low, grad_low_t, normed_t, pre, updown, deps):
    rows, width = grad_low.shape
    parts, _, cols = updown.shape
    cols = cols // 2
    up_part = pl.BlockSpec((1, width, cols), lambda t: (t, 0, 0))
    down_part = pl.BlockSpec((1, width, cols), lambda t: (t, 0, 1))
    return pl.pallas_call(
        skip_deps(feed_backward_body, 6, len(deps)),
        grid=(parts,),
        in_specs=[
            whole_spec((rows, width)), whole_spec((width, rows)), whole_spec((width, rows)),
            pl.BlockSpec((1, rows, cols), lambda t: (t, 0, 0)), up_part, down_part,
        ] + dep_specs(deps),
        out_specs=[
            pl.BlockSpec((1, width, 2 * cols), lambda t: (t, 0, 0)),
            pl.BlockSpec((1, 1, cols), lambda t: (t, 0, 0)),
            whole_spec((rows, width)),
        ],
        out_shape=[
            jax.ShapeDtypeStruct((parts, width, 2 * cols), bf16),
            jax.ShapeDtypeStruct((parts, 1, cols), f32),
            jax.ShapeDtypeStruct((rows, width), f32),
        ],
        compiler_params=pltpu.CompilerParams(vmem_limit_bytes=VMEM_BYTES),
        cost_estimate=COST,
        name="feed_backward",
    )(grad_low, grad_low_t, normed_t, pre, updown, updown, *deps)


def norm_stats(values):
    mean = jnp.mean(values, axis=-1, keepdims=True)
    centred = values - mean
    var = jnp.mean(centred * centred, axis=-1, keepdims=True)
    scale = lax.rsqrt(var + eps)
    return centred * scale, scale


def norm_forward(values, gain, shift):
    return (norm_stats(values)[0] * gain + shift).astype(bf16)


def norm_backward(values, gain, grad):
    unit, scale = norm_stats(values)
    inner = grad * gain
    back = scale * (
        inner
        - jnp.mean(inner, axis=-1, keepdims=True)
        - unit * jnp.mean(inner * unit, axis=-1, keepdims=True)
    )
    return back, jnp.sum(grad * unit, axis=0), jnp.sum(grad, axis=0)


def hop(value, axis, move):
    count = lax.axis_size(axis)
    return lax.ppermute(value, axis, [(i, move(i)) for i in range(count)])


def hop_x(value):
    return hop(value, "tp", lambda i: i ^ 2)


def hop_core(value):
    return hop(value, "tp", lambda i: i ^ 1)


def hop_y(value):
    return hop(value, "fsdp", lambda i: i ^ 1)


def hop_z(value, step):
    count = lax.axis_size("fsdp")
    return hop(value, "fsdp", lambda i: (i + 2 * step) % count)


def places():
    fsdp_index, tp_index = lax.axis_index("fsdp"), lax.axis_index("tp")
    return tp_index // 2, tp_index % 2, fsdp_index // 2, fsdp_index % 2


def gather_line(shard):
    deep = lax.axis_size("fsdp") // 2
    z = places()[2]
    arrived = [hop_z(shard, step) for step in range(1, deep)]
    line = lax.dynamic_update_slice(
        jnp.zeros((deep,) + shard.shape, shard.dtype), shard[None], (z,) + (0,) * shard.ndim
    )
    for step, piece in enumerate(arrived, 1):
        line = lax.dynamic_update_slice(line, piece[None], ((z - step) % deep,) + (0,) * shard.ndim)
    return line, arrived


def gather_plane(line):
    deep, rows, cols = line.shape
    x, _, _, y = places()
    half = cols // 2
    by_x, by_y = hop_x(line), hop_y(line)
    first, second = hop_x(by_y[:, :, :half]), hop_y(by_x[:, :, half:])
    mine = jnp.zeros((2, deep, 2, rows, cols), line.dtype)

    def put(whole, piece, at_x, at_y, at_col):
        return lax.dynamic_update_slice(whole, piece[None, :, None], (at_x, 0, at_y, 0, at_col))

    mine = put(mine, line, x, y, 0)
    mine = put(mine, by_x, 1 - x, y, 0)
    mine = put(mine, by_y, x, 1 - y, 0)
    mine = put(mine, first, 1 - x, 1 - y, 0)
    mine = put(mine, second, 1 - x, 1 - y, half)
    return mine.reshape(2, deep * 2 * rows, cols), (by_x, by_y), (first, second)


def gather_small(values):
    deep = lax.axis_size("fsdp") // 2
    x, core, _, y = places()
    line = gather_line(values)[0]

    def both(value, index, move, axis):
        other = move(value)
        pair = jnp.where(index == 0, jnp.stack([value, other]), jnp.stack([other, value]))
        return jnp.moveaxis(pair, 0, axis)

    whole = both(both(both(line, y, hop_y, 1), x, hop_x, 2), core, hop_core, 3)
    return whole.reshape(deep * 8, values.shape[0])


def scatter_small(values):
    deep = lax.axis_size("fsdp") // 2
    x, core, z, y = places()
    left = values.reshape(deep, 2, 2, 2, -1)
    for index, move, axis in ((core, hop_core, 3), (x, hop_x, 2), (y, hop_y, 1)):
        left = pick(left, index, axis) + move(pick(left, 1 - index, axis))
    arrived = [hop_z(pick(left, (z + step) % deep, 0), step) for step in range(1, deep)]
    return sum(arrived, pick(left, z, 0))


def add_low(left, right):
    return (left.astype(f32) + right.astype(f32)).astype(bf16)


def pick(value, index, axis):
    return lax.dynamic_index_in_dim(value, index, axis, keepdims=False)


class Scatter:
    def __init__(self, other):
        self.parts, self.rest = [hop_core(other)], None

    def keep(self, mine):
        deep = lax.axis_size("fsdp") // 2
        cols = mine.shape[2]
        self.rest = add_low(mine, self.parts[0]).reshape(2, deep, 2, -1, cols)
        x, _, _, y = places()
        half = cols // 2
        self.left, self.right = self.rest[..., :half], self.rest[..., half:]
        self.parts = [hop_x(pick(self.left, 1 - x, 0)), hop_y(pick(self.right, 1 - y, 2))]

    def cross(self):
        x, _, _, y = places()
        self.left = add_low(pick(self.left, x, 0), self.parts[0])
        self.right = add_low(pick(self.right, y, 2), self.parts[1])
        self.parts = [hop_y(pick(self.left, 1 - y, 1)), hop_x(pick(self.right, 1 - x, 0))]

    def along(self):
        deep = lax.axis_size("fsdp") // 2
        x, _, z, y = places()
        left = add_low(pick(self.left, y, 1), self.parts[0])
        right = add_low(pick(self.right, x, 0), self.parts[1])
        self.line = jnp.concatenate([left, right], axis=2)
        self.parts = [
            hop_z(pick(self.line, (z + step) % deep, 0), step) for step in range(1, deep)
        ]

    def total(self):
        total = pick(self.line, places()[2], 0).astype(f32)
        for piece in self.parts:
            total = total + piece.astype(f32)
        return total


def from_previous(rows):
    tp = lax.axis_size("tp")
    return lax.ppermute(rows, "tp", [(i, i + 1) for i in range(tp - 1)])


def to_previous(rows):
    tp = lax.axis_size("tp")
    return lax.ppermute(rows, "tp", [(i + 1, i) for i in range(tp - 1)])


def side_by_side(parts):
    return jnp.concatenate([parts[t] for t in range(parts.shape[0])], axis=1)


def apart(whole, parts):
    cols = whole.shape[1] // parts
    return [whole[:, t * cols : (t + 1) * cols] for t in range(parts)]


def on_device(
    tokens, cotangent, lengths, w_query, w_key, w_value, w_out, w_up, w_down,
    norm_gain, norm_shift, attn_bias, up_bias, down_bias,
):
    fsdp, tp = lax.axis_size("fsdp"), lax.axis_size("tp")
    devices = fsdp * tp
    tp_index = lax.axis_index("tp")
    rows, width = tokens.shape
    layers = w_query.shape[0]
    head_cols, hidden_cols = w_query.shape[2], w_up.shape[2]

    smalls = [norm_gain, norm_shift, attn_bias, up_bias, down_bias]
    packed_all = gather_small(jnp.concatenate([part.reshape(-1) for part in smalls]))
    wholes, at = [], 0
    for part in smalls:
        size, lead, last = part.size, part.shape[:-1], part.shape[-1]
        piece = packed_all[:, at : at + size].reshape((devices,) + part.shape)
        wholes.append(jnp.moveaxis(piece, 0, -2).reshape(lead + (devices * last,)))
        at += size
    gain_all, shift_all, bias_attn, bias_up, bias_down = wholes

    shards = []
    for layer in range(layers):
        shards.append(
            jnp.concatenate([w_query[layer], w_key[layer], w_value[layer], w_out[layer].T], axis=1)
        )
        shards.append(jnp.concatenate([w_up[layer], w_down[layer].T], axis=1))
    lines, planes = [], []
    for number, shard in enumerate(shards):
        lines.append(gather_line(tie(shard, lines[-1][1]) if number else shard))
    for number, (line, _) in enumerate(lines):
        planes.append(gather_plane(tie(line, planes[-1][2]) if number else line))
    weights = [(mine, hop_core(mine)) for mine, _, _ in planes]

    _, core, _, _ = places()

    def core_order(values, cols):
        lead = values.shape[:-1]
        split = values.reshape(lead + (2, 2, cols))
        return jnp.stack([pick(split, core, -2), pick(split, 1 - core, -2)], axis=len(lead))

    def part_order(values, cols):
        split = values.reshape(2, 2, cols)
        split = jnp.stack([pick(split, core, 0), pick(split, 1 - core, 0)], axis=1)
        return split.reshape(-1)

    bias_query = core_order(bias_attn[:, 0], head_cols).reshape(layers, width)
    bias_value = core_order(bias_attn[:, 1], head_cols).reshape(layers, width)
    bias_hidden = core_order(bias_up, hidden_cols)[:, :, :, None]

    seq_ends = jnp.cumsum(lengths[0])
    first_row = tp_index * rows
    key_ids = first_row - rows + jnp.arange(2 * rows, dtype=jnp.int32)
    segments = jnp.sum((key_ids[:, None] >= seq_ends[None, :]).astype(jnp.int32), axis=1)
    segments = jnp.where(key_ids >= 0, segments, -1)
    seg_q, seg_k = segments[rows:, None], segments[None, :]

    stream = tokens.astype(f32)
    saved = []
    for layer in range(layers):
        attn_w, feed_w = jnp.concatenate(weights[2 * layer], axis=0), weights[2 * layer + 1]
        later = 2 * layer + 2
        ahead = [[], [], []]
        if layer + 1 < layers:
            ahead = [lines[later][1], lines[later + 1][1], planes[later][1]]
        wq, wk, wv, wo = (
            side_by_side(attn_w[:, :, n * head_cols : (n + 1) * head_cols]) for n in range(4)
        )
        normed = norm_forward(stream, gain_all[layer, 0], shift_all[layer, 0])
        wide = jnp.concatenate([from_previous(normed), normed], axis=0)
        queries = (dot_nn(normed, wq) + bias_query[layer]).astype(bf16)
        keys = dot_nn(wide, wk).astype(bf16)
        values = (dot_nn(wide, wv) + bias_value[layer]).astype(bf16)
        attended, lse = attend_forward(seg_q, seg_k, queries, keys, values, ahead[0])
        if layer:
            attended = tie(attended, planes[2 * layer + 1][1])
        mid = stream + dot_nt(attended, wo) + bias_attn[layer, 2]
        normed_mid = norm_forward(mid, gain_all[layer, 1], shift_all[layer, 1])
        pre_mine, fed_mine = feed_forward(normed_mid, feed_w[0], bias_hidden[layer, 0], ahead[1])
        pre_other, fed_other = feed_forward(normed_mid, feed_w[1], bias_hidden[layer, 1], ahead[2])
        saved.append(
            (stream, wide, queries, keys, values, attended, lse, mid, normed_mid, pre_mine,
             pre_other, wq, wk, wv, wo)
        )
        stream = mid + fed_mine + fed_other + bias_down[layer]

    grad = cotangent.astype(f32)
    small_grads = [None] * layers
    feed_sums, attn_sums = [], []
    for layer in reversed(range(layers)):
        feed_w = weights[2 * layer + 1]
        top = layer + 1 == layers
        (stream_in, wide, queries, keys, values, attended, lse, mid, normed_mid, pre_mine, pre_other,
         wq, wk, wv, wo) = saved[layer]
        normed = wide[rows:]
        grad_bias_down = jnp.sum(grad, axis=0)
        grad_low = grad.astype(bf16)
        turned = (grad_low, grad_low.T, normed_mid.T)
        deps = [] if top else feed_sums[-1].parts
        grad_other, grad_bias_other, dn_other = feed_backward(*turned, pre_other, feed_w[1], deps)
        if not top:
            feed_sums[-1].along()
        feed_sum = Scatter(grad_other)
        deps = [] if top else attn_sums[-1].parts
        grad_mine, grad_bias_mine, dn_mine = feed_backward(*turned, pre_mine, feed_w[0], deps)
        if not top:
            attn_sums[-1].keep(attn_mine)
        feed_sum.keep(grad_mine)
        feed_sums.append(feed_sum)
        dn = dn_mine + dn_other
        grad_bias_up = jnp.stack([grad_bias_mine, grad_bias_other])
        back, gain_second, shift_second = norm_backward(mid, gain_all[layer, 1], dn)
        grad = grad + back
        grad_bias_out = jnp.sum(grad, axis=0)
        grad_low = grad.astype(bf16)
        grad_wo = dot_tn(grad_low, attended).astype(bf16)
        grad_attended = dot_nn(grad_low, wo).astype(bf16)
        deps = [] if top else attn_sums[-1].parts + feed_sums[-2].parts
        dq, dk, dv = attend_backward(
            seg_q, seg_k, queries, keys, values, attended, lse, grad_attended, deps
        )
        if not top:
            attn_sums[-1].cross()
        dk = tie(dk, feed_sum.parts)
        feed_sum.cross()
        if not top:
            dv = tie(dv, attn_sums[-1].parts)
            attn_sums[-1].along()
        dn_wide = dot_nt(dk, wk) + dot_nt(dv, wv)
        dn_before = to_previous(dn_wide[:rows].astype(bf16)).astype(f32)
        grad_wq = dot_tn(normed, dq).astype(bf16)
        grad_wk = dot_tn(wide, dk).astype(bf16)
        grad_wv = dot_tn(wide, dv).astype(bf16)
        grad_attn = jnp.stack(
            [
                jnp.concatenate(four, axis=1)
                for four in zip(*(apart(whole, tp) for whole in (grad_wq, grad_wk, grad_wv, grad_wo)))
            ]
        )
        attn_mine = grad_attn[: tp // 2]
        attn_sums.append(Scatter(grad_attn[tp // 2 :]))
        dn = dn_wide[rows:] + dot_nt(dq, wq) + dn_before
        back, gain_first, shift_first = norm_backward(stream_in, gain_all[layer, 0], dn)
        grad = grad + back
        small_grads[layer] = (
            jnp.stack([gain_first, gain_second]),
            jnp.stack([shift_first, shift_second]),
            jnp.stack(
                [
                    part_order(jnp.sum(dq.astype(f32), axis=0), head_cols),
                    part_order(jnp.sum(dv.astype(f32), axis=0), head_cols),
                    grad_bias_out,
                ]
            ),
            part_order(grad_bias_up, hidden_cols),
            grad_bias_down,
        )

    pieces = []
    for member, part in enumerate(smalls):
        whole = jnp.stack([small_grads[layer][member] for layer in range(layers)])
        last = part.shape[-1]
        split = whole.reshape(part.shape[:-1] + (devices, last))
        pieces.append(jnp.moveaxis(split, -2, 0).reshape(devices, part.size))
    summed = scatter_small(jnp.concatenate(pieces, axis=1))[None]

    feed_sums[-1].along()
    attn_sums[-1].keep(attn_mine)
    attn_sums[-1].cross()
    attn_sums[-1].along()
    shards = [None] * layers
    for layer in range(layers):
        attn_shard = attn_sums[layers - 1 - layer].total()
        feed_shard = feed_sums[layers - 1 - layer].total()
        shards[layer] = tuple(attn_shard[:, n * head_cols : (n + 1) * head_cols] for n in range(3)) + (
            attn_shard[:, 3 * head_cols :].T, feed_shard[:, :hidden_cols], feed_shard[:, hidden_cols:].T,
        )
    small_outs, at = [], 0
    for part in smalls:
        small_outs.append(summed[:, at : at + part.size].reshape(part.shape))
        at += part.size
    stacked = [jnp.stack([shards[layer][n] for layer in range(layers)]) for n in range(6)]
    return (stream.astype(bf16), grad, *stacked, *small_outs)


def solution(mesh):
    tokens_spec = P(BOTH, None)
    in_spec, out_spec = P(None, "fsdp", "tp"), P(None, "tp", "fsdp")
    matrices = (in_spec, in_spec, in_spec, out_spec, in_spec, out_spec)
    smalls = (P(None, None, BOTH),) * 3 + (P(None, BOTH),) * 2
    return jax.shard_map(
        on_device,
        mesh=mesh,
        in_specs=(tokens_spec, tokens_spec, P("fsdp", None)) + matrices + smalls,
        out_specs=(tokens_spec, tokens_spec) + matrices + smalls,
        check_vma=False,
    )
```

```python
import functools

import jax
import jax.numpy as jnp
from jax import lax
from jax.experimental import pallas as pl
from jax.experimental.pallas import tpu as pltpu
from jax.sharding import PartitionSpec as P

HEAD = 64
QROWS = 256
QROWS_FORWARD = 256
eps = 1e-05
masked_fill = -1e30
VMEM_BYTES = 56 * 1024 * 1024
BOTH = ("fsdp", "tp")

f32 = jnp.float32
bf16 = jnp.bfloat16


def dot_nn(left, right):
    return lax.dot_general(left, right, (((1,), (0,)), ((), ())), preferred_element_type=f32)


def dot_nt(left, right):
    return lax.dot_general(left, right, (((1,), (1,)), ((), ())), preferred_element_type=f32)


def dot_tn(left, right):
    return lax.dot_general(left, right, (((0,), (0,)), ((), ())), preferred_element_type=f32)


def tie(value, deps):
    deps = list(deps)
    if not deps:
        return value
    return pl.pallas_call(
        lambda *refs: None,
        in_specs=[pl.BlockSpec(memory_space=pl.ANY)] * (1 + len(deps)),
        out_specs=pl.BlockSpec(memory_space=pl.ANY),
        out_shape=jax.ShapeDtypeStruct(value.shape, value.dtype),
        input_output_aliases={0: 0},
        name="tie",
    )(value, *deps)


def dep_specs(deps):
    return [pl.BlockSpec(memory_space=pl.ANY)] * len(deps)


def skip_deps(body, inputs, count):
    return lambda *refs: body(*refs[:inputs], *refs[inputs + count :])


def cost_of(products):
    return pl.CostEstimate(flops=2 * products * 512**3, bytes_accessed=1000, transcendentals=0)


COSTS = dict(
    attend_forward=16, attend_backward=26, feed_forward=9, feed_backward=14, norm_forward=3, norm_backward=6,
    stack_small=2
)


TILE = 2 * HEAD
PROJECTED = 5 * TILE
TILE_A, TILE_B, TILE_C, TILE_D, TILE_E = (slice(n * TILE, (n + 1) * TILE) for n in range(5))
FIRST, SECOND = slice(0, TILE), slice(TILE, 2 * TILE)
HEADS_OF_PART = (
    (TILE_A, TILE_B, TILE_C, 0, 0, SECOND),
    (TILE_A, TILE_B, TILE_C, 1, 1, SECOND),
    (TILE_D, TILE_E, TILE_D, 0, 1, FIRST),
)


def fill_bias(seg_q_ref, seg_k_ref, bias_ref, rows, block):
    window = rows + block
    for first in range(0, rows, block):
        row_pos = rows + first + lax.broadcasted_iota(jnp.int32, (block, window), 0)
        col_pos = first + lax.broadcasted_iota(jnp.int32, (block, window), 1)
        same = seg_q_ref[first : first + block, :] == seg_k_ref[:, first : first + window]
        bias_ref[first : first + block, :] = jnp.where(same & (col_pos <= row_pos), 0.0, masked_fill)


def fill_bias_turned(seg_q_ref, seg_k_ref, bias_ref, rows, block):
    window = rows + block
    for first in range(0, rows, block):
        row_pos = rows + first + lax.broadcasted_iota(jnp.int32, (window, block), 1)
        col_pos = first + lax.broadcasted_iota(jnp.int32, (window, block), 0)
        same = seg_q_ref[:, first : first + block] == seg_k_ref[first : first + window, :]
        bias_ref[first // block] = jnp.where(same & (col_pos <= row_pos), 0.0, masked_fill)


def halves(block):
    low = lax.broadcasted_iota(jnp.int32, (block, TILE), 1) < HEAD
    return low, ~low


def attend_forward_body(
    rows, seg_q_ref, seg_k_ref, halo_ref, own_ref, w_ref, b_ref, acc_ref, row_ref,
    p_ref, att_ref, lse_ref, out_ref, bias_ref,
):
    window = rows + QROWS_FORWARD

    @pl.when(pl.program_id(0) == 0)
    def _():
        fill_bias(seg_q_ref, seg_k_ref, bias_ref, rows, QROWS_FORWARD)
        out_ref[...] = acc_ref[...] + row_ref[...]

    weight = w_ref[0, :, :PROJECTED]
    p_ref[0, :rows] = (dot_nn(halo_ref[...], weight) + b_ref[0]).astype(bf16)
    p_ref[0, rows:] = (dot_nn(own_ref[...], weight) + b_ref[0]).astype(bf16)
    half = halves(QROWS_FORWARD)
    for first in range(0, rows, QROWS_FORWARD):
        here = slice(first, first + QROWS_FORWARD)
        own = slice(rows + first, rows + first + QROWS_FORWARD)
        span = slice(first, first + window)
        bias = bias_ref[here, :]
        outs, lses = [], []
        for q_tile, k_tile, v_tile, q_half, _, _ in HEADS_OF_PART:
            queries = jnp.where(half[q_half], p_ref[0, own, q_tile] * jnp.asarray(HEAD**-0.5, bf16), 0)
            scores = dot_nt(queries, p_ref[0, span, k_tile]) + bias
            top = jnp.max(scores, axis=-1, keepdims=True)
            terms = jnp.exp(scores - top)
            total = jnp.sum(terms, axis=-1, keepdims=True)
            outs.append(dot_nn(terms.astype(bf16), p_ref[0, span, v_tile]) * (1.0 / total))
            lses.append(top + jnp.log(total))
        att_ref[0, here, FIRST] = jnp.where(half[0], 0.0, outs[2]).astype(bf16)
        att_ref[0, here, SECOND] = jnp.where(half[0], outs[0], outs[1]).astype(bf16)
        lse_ref[0, here, FIRST] = jnp.broadcast_to(lses[2], (QROWS_FORWARD, TILE))
        lse_ref[0, here, SECOND] = jnp.where(half[0], lses[0], lses[1])
    out_ref[...] += dot_nt(att_ref[0], w_ref[0, :, 4 * TILE :])


def attend_backward_body(
    rows, first_call, seg_q_ref, seg_k_ref, g_ref, halo_ref, own_ref, w_ref, p_ref, att_ref, lse_ref,
    acc_ref, gw_ref, gb_ref, dn_ref, low_ref, bias_ref, dp_ref,
):
    window = rows + QROWS

    @pl.when(pl.program_id(0) == 0)
    def _():
        fill_bias_turned(seg_q_ref, seg_k_ref, bias_ref, rows, QROWS)
        if first_call:
            dn_ref[...] = jnp.zeros_like(dn_ref)
        else:
            dn_ref[...] = acc_ref[...]

    dp_ref[...] = jnp.zeros_like(dp_ref)
    grads = dot_nn(g_ref[...], w_ref[0, :, 4 * TILE :]).astype(bf16)
    half = halves(QROWS)
    for first in range(0, rows, QROWS):
        here = slice(first, first + QROWS)
        own = slice(rows + first, rows + first + QROWS)
        span = slice(first, first + window)
        bias = bias_ref[first // QROWS]
        lses = [lse_ref[0, here, tile].T for tile in (FIRST, SECOND)]
        products = [
            (grads[here, tile].astype(f32) * att_ref[0, here, tile].astype(f32)).T
            for tile in (FIRST, SECOND)
        ]
        dqs = []
        for head, (q_tile, k_tile, v_tile, q_half, v_half, a_tile) in enumerate(HEADS_OF_PART):
            queries = jnp.where(half[q_half], p_ref[0, own, q_tile] * jnp.asarray(HEAD**-0.5, bf16), 0)
            keys = p_ref[0, span, k_tile]
            grad = jnp.where(half[v_half], grads[here, a_tile], 0)
            which = 0 if a_tile == FIRST else 1
            lanes = slice(v_half * HEAD, v_half * HEAD + HEAD)
            inner = jnp.sum(products[which][lanes], axis=0, keepdims=True)
            lse = lses[which][v_half * HEAD : v_half * HEAD + 1]
            probs = jnp.exp(dot_nt(keys, queries) + bias - lse)
            draw = (probs * (dot_nt(p_ref[0, span, v_tile], grad) - inner)).astype(bf16)
            dp_ref[span, v_tile] += dot_nn(probs.astype(bf16), grad)
            dp_ref[span, k_tile] += dot_nn(draw, queries)
            dqs.append(dot_tn(draw, keys))
        dp_ref[own, TILE_A] = jnp.where(half[0], dqs[0], dqs[1]) * HEAD**-0.5
        dp_ref[own, TILE_D] += jnp.where(half[0], dqs[2], 0.0) * HEAD**-0.5
    dp = dp_ref[...].astype(bf16)
    gb_ref[0, :, :PROJECTED] = jnp.sum(dp.astype(f32), axis=0, keepdims=True)
    gb_ref[0, :, PROJECTED:] = jnp.zeros((1, gb_ref.shape[2] - PROJECTED), f32)
    halo_dp, own_dp = dp[:rows], dp[rows:]
    by_rows = dot_tn(halo_ref[...], halo_dp) + dot_tn(own_ref[...], own_dp)
    shared = dot_tn(g_ref[...], att_ref[0])
    gw_ref[0, :, : 4 * TILE] = by_rows[:, : 4 * TILE].astype(bf16)
    gw_ref[0, :, TILE_E] = (by_rows[:, TILE_E] + shared[:, FIRST]).astype(bf16)
    gw_ref[0, :, 5 * TILE :] = shared[:, SECOND].astype(bf16)
    dn_ref[...] += dot_nt(dp, w_ref[0, :, :PROJECTED])

    @pl.when(pl.program_id(0) == pl.num_programs(0) - 1)
    def _():
        low_ref[...] = dn_ref[:rows].astype(bf16)


def whole_spec(shape):
    return pl.BlockSpec(shape, lambda *_: (0,) * len(shape))


def part_spec(shape):
    return pl.BlockSpec((1,) + shape, lambda t: (t, 0, 0))


def call_parts(body, parts, ins, outs, scratch, name, operands, deps):
    deps = list(deps)
    in_specs = [
        part_spec(value.shape[1:]) if split else whole_spec(value.shape)
        for value, split in zip(operands, ins)
    ]
    return pl.pallas_call(
        skip_deps(body, len(operands), len(deps)),
        grid=(parts,),
        in_specs=in_specs + dep_specs(deps),
        out_specs=[part_spec(shape[1:]) if split else whole_spec(shape) for shape, _, split in outs],
        out_shape=[jax.ShapeDtypeStruct(shape, dtype) for shape, dtype, _ in outs],
        scratch_shapes=scratch,
        compiler_params=pltpu.CompilerParams(vmem_limit_bytes=VMEM_BYTES),
        cost_estimate=cost_of(COSTS[name]),
        name=name,
    )(*operands, *deps)


def attend_forward(seg_q, seg_k, halo, own, weight, bias, acc, row, deps=()):
    parts, width, _ = weight.shape
    rows = own.shape[0]
    return call_parts(
        functools.partial(attend_forward_body, rows),
        parts,
        (False, False, False, False, True, True, False, False),
        [
            ((parts, 2 * rows, PROJECTED), bf16, True),
            ((parts, rows, 2 * TILE), bf16, True),
            ((parts, rows, 2 * TILE), f32, True),
            ((rows, width), f32, False),
        ],
        [pltpu.VMEM((rows, rows + QROWS_FORWARD), f32)],
        "attend_forward",
        (seg_q, seg_k, halo, own, weight, bias, acc, row),
        deps,
    )


def attend_backward(seg_q, seg_k, grad, halo, own, weight, projected, attended, lse, acc, deps=()):
    parts, width, cols = weight.shape
    rows = grad.shape[0]
    first_call = acc is None
    return call_parts(
        functools.partial(attend_backward_body, rows, first_call),
        parts,
        (False, False, False, False, False, True, True, True, True, False),
        [
            ((parts, width, cols), bf16, True),
            ((parts, 1, cols), f32, True),
            ((2 * rows, width), f32, False),
            ((rows, width), bf16, False),
        ],
        [
            pltpu.VMEM((rows // QROWS, rows + QROWS, QROWS), f32),
            pltpu.VMEM((2 * rows, PROJECTED), f32),
        ],
        "attend_backward",
        (seg_q, seg_k, grad, halo, own, weight, projected, attended, lse, seg_q if first_call else acc),
        deps,
    )


GELU_A = 0.7978845608028654
GELU_B = 0.044715


def gelu_parts(pre):
    square = pre * pre
    bend = jnp.tanh(GELU_A * pre * (1.0 + GELU_B * square))
    half = 0.5 * (1.0 + bend)
    slope = half + 0.5 * pre * (1.0 - bend * bend) * (GELU_A * (1.0 + 3.0 * GELU_B * square))
    return pre * half, slope


def feed_forward_body(n_ref, w_ref, bias_ref, acc_ref, row_ref, pre_ref, out_ref):
    @pl.when(pl.program_id(0) == 0)
    def _():
        out_ref[...] = acc_ref[...] + row_ref[...]

    cols = pre_ref.shape[2]
    pre = dot_nn(n_ref[...], w_ref[0, :, :cols]) + bias_ref[0]
    pre_ref[0] = pre
    hidden = gelu_parts(pre)[0].astype(bf16)
    out_ref[...] += dot_nt(hidden, w_ref[0, :, cols:])


def feed_forward(normed, weight, bias, acc, row, deps=()):
    rows, width = normed.shape
    parts, _, cols = weight.shape
    return call_parts(
        feed_forward_body,
        parts,
        (False, True, True, False, False),
        [((parts, rows, cols // 2), f32, True), ((rows, width), f32, False)],
        [],
        "feed_forward",
        (normed, weight, bias, acc, row),
        deps,
    )


def feed_backward_body(first_call, g_ref, n_ref, pre_ref, w_ref, acc_ref, gw_ref, gbias_ref, dn_ref):
    @pl.when(pl.program_id(0) == 0)
    def _():
        if first_call:
            dn_ref[...] = jnp.zeros_like(dn_ref)
        else:
            dn_ref[...] = acc_ref[...]

    hidden, slope = gelu_parts(pre_ref[0])
    cols = hidden.shape[1]
    gw_ref[0, :, cols:] = dot_tn(g_ref[...], hidden.astype(bf16)).astype(bf16)
    dpre = (dot_nn(g_ref[...], w_ref[0, :, cols:]) * slope).astype(bf16)
    gbias_ref[0] = jnp.sum(dpre.astype(f32), axis=0, keepdims=True)
    gw_ref[0, :, :cols] = dot_tn(n_ref[...], dpre).astype(bf16)
    dn_ref[...] += dot_nt(dpre, w_ref[0, :, :cols])


def feed_backward(grad, normed, pre, weight, acc, deps=()):
    rows, width = normed.shape
    parts, _, cols = weight.shape
    first_call = acc is None
    return call_parts(
        functools.partial(feed_backward_body, first_call),
        parts,
        (False, False, True, True, False),
        [
            ((parts, width, cols), bf16, True),
            ((parts, 1, cols // 2), f32, True),
            ((rows, width), f32, False),
        ],
        [],
        "feed_backward",
        (grad, normed, pre, weight, normed if first_call else acc),
        deps,
    )


def norm_stats(values):
    mean = jnp.mean(values, axis=-1, keepdims=True)
    centred = values - mean
    var = jnp.mean(centred * centred, axis=-1, keepdims=True)
    scale = lax.rsqrt(var + eps)
    return centred * scale, scale


def norm_forward_body(x_ref, gain_ref, shift_ref, out_ref):
    out_ref[...] = (norm_stats(x_ref[...])[0] * gain_ref[...] + shift_ref[...]).astype(bf16)


def call_whole(body, outs, name, operands, deps=()):
    deps = list(deps)
    return pl.pallas_call(
        skip_deps(body, len(operands), len(deps)),
        in_specs=[pl.BlockSpec(memory_space=pltpu.VMEM)] * len(operands) + dep_specs(deps),
        out_specs=[pl.BlockSpec(memory_space=pltpu.VMEM)] * len(outs),
        out_shape=[jax.ShapeDtypeStruct(shape, dtype) for shape, dtype in outs],
        compiler_params=pltpu.CompilerParams(vmem_limit_bytes=VMEM_BYTES),
        cost_estimate=cost_of(COSTS[name]),
        name=name,
    )(*operands, *deps)


def norm_forward(values, gain, shift):
    return call_whole(
        norm_forward_body, [(values.shape, bf16)], "norm_forward", (values, gain[None], shift[None])
    )[0]


def norm_backward_body(x_ref, gain_ref, dn_ref, more_ref, g_ref, out_ref, low_ref, sums_ref):
    unit, scale = norm_stats(x_ref[...])
    rows = x_ref.shape[0]
    grad = dn_ref[dn_ref.shape[0] - rows :, :]
    if more_ref is not None:
        grad = grad + more_ref[...].astype(f32)
    inner = grad * gain_ref[...]
    back = scale * (
        inner
        - jnp.mean(inner, axis=-1, keepdims=True)
        - unit * jnp.mean(inner * unit, axis=-1, keepdims=True)
    )
    total = g_ref[...] + back
    out_ref[...] = total
    low_ref[...] = total.astype(bf16)
    sums_ref[0:1] = jnp.sum(grad * unit, axis=0, keepdims=True)
    sums_ref[1:2] = jnp.sum(grad, axis=0, keepdims=True)
    sums_ref[2:3] = jnp.sum(total, axis=0, keepdims=True)


def norm_backward(values, gain, dn, more, grad, deps=()):
    rows, width = values.shape
    outs = [((rows, width), f32), ((rows, width), bf16), ((3, width), f32)]
    if more is None:
        return call_whole(
            lambda x, gain, dn, *rest: norm_backward_body(x, gain, dn, None, *rest),
            outs, "norm_backward", (values, gain[None], dn, grad), deps,
        )
    return call_whole(norm_backward_body, outs, "norm_backward", (values, gain[None], dn, more, grad), deps)


def stack_small_body(core_ref, *refs):
    *row_refs, out_ref = refs
    out_ref[...] = jnp.zeros_like(out_ref)
    first = core_ref[...] == 0
    out_ref[0:1] = row_refs[0][...]
    at = 1
    for start in range(1, len(row_refs), 6):
        proj_mine, proj_other, up_mine, up_other, mid, before = row_refs[start : start + 6]
        for mine, other in ((proj_mine, proj_other), (up_mine, up_other)):
            for part in range(2):
                out_ref[at + part : at + part + 1] = jnp.where(first, mine[part], other[part])
                out_ref[at + 2 + part : at + 3 + part] = jnp.where(first, other[part], mine[part])
            at += 4
        out_ref[at : at + 3] = mid[...]
        out_ref[at + 3 : at + 6] = before[...]
        at += 6


def stack_small(core, rows):
    count = 1 + 14 * (len(rows) // 6)
    shape = (-(-count // 8) * 8, rows[0].shape[1])
    return call_whole(stack_small_body, [(shape, f32)], "stack_small", (core.reshape(1, 1), *rows))[0]


def hop(value, axis, move):
    count = lax.axis_size(axis)
    return lax.ppermute(value, axis, [(i, move(i)) for i in range(count)])


def hop_x(value):
    return hop(value, "tp", lambda i: i ^ 2)


def hop_core(value):
    return hop(value, "tp", lambda i: i ^ 1)


def hop_y(value):
    return hop(value, "fsdp", lambda i: i ^ 1)


def hop_z(value, step):
    count = lax.axis_size("fsdp")
    return hop(value, "fsdp", lambda i: (i + 2 * step) % count)


def places():
    fsdp_index, tp_index = lax.axis_index("fsdp"), lax.axis_index("tp")
    return tp_index // 2, tp_index % 2, fsdp_index // 2, fsdp_index % 2


def gather_line(shard):
    deep = lax.axis_size("fsdp") // 2
    z = places()[2]
    arrived = [hop_z(shard, step) for step in range(1, deep)]
    line = lax.dynamic_update_slice(
        jnp.zeros((deep,) + shard.shape, shard.dtype), shard[None], (z,) + (0,) * shard.ndim
    )
    for step, piece in enumerate(arrived, 1):
        line = lax.dynamic_update_slice(line, piece[None], ((z - step) % deep,) + (0,) * shard.ndim)
    return line, arrived


class Gather:
    def __init__(self, shard, after=()):
        self.line, self.parts = gather_line(tie(shard, after))

    def cross(self, after=()):
        self.line = tie(self.line, after)
        self.parts = [hop_x(self.line), hop_y(self.line)]

    def relay(self, after=()):
        half = self.line.shape[2] // 2
        self.by_x, self.by_y = (tie(part, after) for part in self.parts)
        self.parts = [hop_x(self.by_y[:, :, :half]), hop_y(self.by_x[:, :, half:])]

    def both_cores(self):
        deep, rows, cols = self.line.shape
        x, _, _, y = places()
        mine = jnp.zeros((2, deep, 2, rows, cols), self.line.dtype)
        for piece, at_x, at_y, at_col in (
            (self.line, x, y, 0),
            (self.by_x, 1 - x, y, 0),
            (self.by_y, x, 1 - y, 0),
            (self.parts[0], 1 - x, 1 - y, 0),
            (self.parts[1], 1 - x, 1 - y, cols // 2),
        ):
            mine = lax.dynamic_update_slice(mine, piece[None, :, None], (at_x, 0, at_y, 0, at_col))
        mine = mine.reshape(2, deep * 2 * rows, cols)
        return mine, hop_core(mine)


def gather_small(values):
    deep = lax.axis_size("fsdp") // 2
    x, core, _, y = places()
    line = gather_line(values)[0]

    def both(value, index, move, axis):
        other = move(value)
        pair = jnp.where(index == 0, jnp.stack([value, other]), jnp.stack([other, value]))
        return jnp.moveaxis(pair, 0, axis)

    whole = both(both(both(line, y, hop_y, 1), x, hop_x, 2), core, hop_core, 3)
    return whole.reshape(deep * 8, values.shape[0])


def sum_small(values):
    deep = lax.axis_size("fsdp") // 2
    for move in (hop_core, hop_x, hop_y):
        values = values + move(values)
    return sum((hop_z(values, step) for step in range(1, deep)), values)


def add_low(*values):
    return sum(value.astype(f32) for value in values).astype(bf16)


def pick(value, index, axis):
    return lax.dynamic_index_in_dim(value, index, axis, keepdims=False)


class Scatter:
    def __init__(self, other):
        self.parts = [hop_core(other)]

    def keep(self, mine):
        deep = lax.axis_size("fsdp") // 2
        x, _, _, y = places()
        cols = mine.shape[2]
        half = cols // 2
        both = [part.reshape(2, deep, 2, -1, cols) for part in (mine, self.parts[0])]
        self.left, self.right = [part[..., :half] for part in both], [part[..., half:] for part in both]
        self.sends = [
            add_low(*(pick(part, 1 - x, 0) for part in self.left)),
            add_low(*(pick(part, 1 - y, 2) for part in self.right)),
        ]
        self.parts = [hop_x(self.sends[0]), hop_y(self.sends[1])]

    def cross(self, after=()):
        x, _, _, y = places()
        by_x, by_y = (tie(part, after) for part in self.parts)
        self.left = add_low(*(pick(part, x, 0) for part in self.left), by_x)
        self.right = add_low(*(pick(part, y, 2) for part in self.right), by_y)
        self.parts = [hop_y(pick(self.left, 1 - y, 1)), hop_x(pick(self.right, 1 - x, 0))]

    def along(self, after=()):
        deep = lax.axis_size("fsdp") // 2
        x, _, z, y = places()
        by_y, by_x = (tie(part, after) for part in self.parts)
        left = add_low(pick(self.left, y, 1), by_y)
        right = add_low(pick(self.right, x, 0), by_x)
        self.line = jnp.concatenate([left, right], axis=2)
        self.parts = [
            hop_z(pick(self.line, (z + step) % deep, 0), step) for step in range(1, deep)
        ]

    def total(self, after=()):
        total = pick(self.line, places()[2], 0).astype(f32)
        for piece in (tie(part, after) for part in self.parts):
            total = total + piece.astype(f32)
        return total


def from_previous(rows):
    tp = lax.axis_size("tp")
    return lax.ppermute(rows, "tp", [(i, i + 1) for i in range(tp - 1)])


def to_previous(rows):
    tp = lax.axis_size("tp")
    return lax.ppermute(rows, "tp", [(i + 1, i) for i in range(tp - 1)])


def on_device(
    tokens, cotangent, lengths, w_query, w_key, w_value, w_out, w_up, w_down,
    norm_gain, norm_shift, attn_bias, up_bias, down_bias,
):
    fsdp, tp = lax.axis_size("fsdp"), lax.axis_size("tp")
    devices = fsdp * tp
    tp_index = lax.axis_index("tp")
    rows, width = tokens.shape
    layers = w_query.shape[0]
    head_cols, hidden_cols = w_query.shape[2], w_up.shape[2]

    def attn_columns(q, k, v, out):
        tiles = [q[:, :TILE], k[:, :TILE], v[:, :TILE], q[:, TILE:], v[:, TILE:], k[:, TILE:]]
        return jnp.concatenate(tiles + [out[:, TILE:], out[:, :TILE]], axis=1)

    def apart(value):
        at = [0, TILE, 2 * TILE, 3 * TILE, 3 * TILE + HEAD, 4 * TILE, 4 * TILE + HEAD, 5 * TILE]
        q, k, v, q2, v2, k2, out2, out = (
            value[:, start:end] for start, end in zip(at, at[1:] + [6 * TILE])
        )
        return [jnp.concatenate(two, axis=1) for two in ((q, q2), (k, k2), (v, v2), (out, out2))]

    shards = []
    for layer in range(layers):
        shards.append(attn_columns(w_query[layer], w_key[layer], w_value[layer], w_out[layer].T))
        shards.append(jnp.concatenate([w_up[layer], w_down[layer].T], axis=1))
    attn = Gather(shards[0])

    smalls = [norm_gain, norm_shift, attn_bias, up_bias, down_bias]
    packed = jnp.concatenate([part.reshape(-1) for part in smalls])
    packed_all = gather_small(tie(packed, attn.parts))
    wholes, at = [], 0
    for part in smalls:
        size, lead, last = part.size, part.shape[:-1], part.shape[-1]
        piece = packed_all[:, at : at + size].reshape((devices,) + part.shape)
        wholes.append(jnp.moveaxis(piece, 0, -2).reshape(lead + (devices * last,)))
        at += size
    gain_all, shift_all, bias_attn, bias_up, bias_down = wholes

    _, core, _, _ = places()

    def core_order(values, cols):
        lead = values.shape[:-1]
        split = values.reshape(lead + (2, 2, cols))
        return jnp.stack([pick(split, core, -2), pick(split, 1 - core, -2)], axis=len(lead))

    def part_order(values, cols):
        split = values.reshape(2, 2, cols)
        split = jnp.stack([pick(split, core, 0), pick(split, 1 - core, 0)], axis=1)
        return split.reshape(-1)

    bias_q = core_order(bias_attn[:, 0], head_cols)
    bias_v = core_order(bias_attn[:, 1], head_cols)
    none = jnp.zeros(bias_q.shape[:-1] + (TILE,), f32)
    bias_proj = jnp.concatenate(
        [bias_q[..., :TILE], none, bias_v[..., :TILE], bias_q[..., TILE:], bias_v[..., TILE:], none],
        axis=-1,
    )[:, :, :, None]
    bias_hidden = core_order(bias_up, hidden_cols)[:, :, :, None]
    no_row = jnp.zeros((1, width), f32)

    seq_ends = jnp.cumsum(lengths[0])
    first_row = tp_index * rows
    key_ids = first_row - rows + jnp.arange(2 * rows, dtype=jnp.int32)
    segments = jnp.sum((key_ids[:, None] >= seq_ends[None, :]).astype(jnp.int32), axis=1)
    segments = jnp.where(key_ids >= 0, segments, -1)
    seg_q, seg_k = segments[rows:, None], segments[None, :]
    turned_q, turned_k = segments[None, rows:], segments[:, None]

    stream = tokens.astype(f32)
    saved, weights = [], []
    feed = Gather(shards[1], attn.parts)
    attn.cross()
    attn.relay()
    feed.cross(attn.parts)
    for layer in range(layers):
        more = layer + 1 < layers
        if more:
            next_attn = Gather(shards[2 * layer + 2], feed.parts + attn.parts)
        normed = norm_forward(stream, gain_all[layer, 0], shift_all[layer, 0])
        halo = from_previous(normed)
        attn_w = attn.both_cores()
        *kept_mine, mid = attend_forward(
            seg_q, seg_k, halo, normed, attn_w[0], bias_proj[layer, 0], stream, bias_attn[layer, 2][None],
            [feed.line],
        )
        *kept_other, mid = attend_forward(
            seg_q, seg_k, halo, normed, attn_w[1], bias_proj[layer, 1], mid, no_row
        )
        feed.relay([mid])
        if more:
            next_feed = Gather(shards[2 * layer + 3], next_attn.parts + [mid])
            next_attn.cross(feed.parts)
        normed_mid = norm_forward(mid, gain_all[layer, 1], shift_all[layer, 1])
        feed_w = feed.both_cores()
        pre_mine, fed = feed_forward(
            normed_mid, feed_w[0], bias_hidden[layer, 0], mid, bias_down[layer][None]
        )
        crossed = []
        if more:
            crossed = next_attn.parts
            next_attn.relay([fed])
            next_feed.cross(next_attn.parts)
        pre_other, fed = feed_forward(
            normed_mid, feed_w[1], bias_hidden[layer, 1], fed, no_row, crossed
        )
        saved.append((stream, halo, normed, kept_mine, kept_other, mid, normed_mid, pre_mine, pre_other))
        weights += [attn_w, feed_w]
        stream = fed
        if more:
            attn, feed = next_attn, next_feed

    grad = cotangent.astype(f32)
    grad_low = cotangent
    small_rows = [jnp.sum(grad, axis=0, keepdims=True)]
    feed_sums, attn_sums = [], []
    for layer in reversed(range(layers)):
        attn_w, feed_w = weights[2 * layer], weights[2 * layer + 1]
        stream_in, halo, normed, kept_mine, kept_other, mid, normed_mid, pre_mine, pre_other = saved[layer]
        before_feed, before_attn = (feed_sums[-1], attn_sums[-1]) if feed_sums else (None, None)
        feed_other, up_other, dn = feed_backward(grad_low, normed_mid, pre_other, feed_w[1], None)
        feed_sum = Scatter(feed_other)
        if before_attn:
            crossed = before_attn.parts
            before_attn.cross([dn])
        feed_mine, up_mine, dn = feed_backward(
            grad_low, normed_mid, pre_mine, feed_w[0], dn,
            before_feed.parts + crossed if before_feed else (),
        )
        relayed = []
        if before_attn:
            relayed = before_attn.parts
            before_attn.along([dn])
        feed_sum.keep(feed_mine)
        grad, grad_low, sums_mid = norm_backward(
            mid, gain_all[layer, 1], dn, None, grad, feed_sum.sends
        )
        attn_other, proj_other, dn, _ = attend_backward(
            turned_q, turned_k, grad_low, halo, normed, attn_w[1], *kept_other, None, relayed
        )
        attn_sum = Scatter(attn_other)
        crossed = feed_sum.parts
        feed_sum.cross([dn])
        attn_mine, proj_mine, dn, dn_halo = attend_backward(
            turned_q, turned_k, grad_low, halo, normed, attn_w[0], *kept_mine, dn,
            crossed + (before_attn.parts if before_attn else []),
        )
        relayed = feed_sum.parts
        feed_sum.along([dn])
        attn_sum.keep(attn_mine)
        grad, grad_low, sums_in = norm_backward(
            stream_in, gain_all[layer, 0], dn, to_previous(dn_halo), grad,
            attn_sum.sends + [feed_sum.line],
        )
        feed_sums.append(feed_sum)
        attn_sums.append(attn_sum)
        small_rows += [proj_mine, proj_other, up_mine, up_other, sums_mid, sums_in]

    summed = sum_small(tie(stack_small(core, small_rows), attn_sums[-1].parts))
    picked, hidden_rows = [], []
    for layer in range(layers):
        at = 1 + 14 * (layers - 1 - layer)
        by_part = summed[at : at + 8].reshape(2, 2, 2, width).swapaxes(1, 2).reshape(2, 4, width)
        proj, up = by_part[0], by_part[1]
        mid, before = summed[at + 8 : at + 11], summed[at + 11 : at + 14]
        grad_q = jnp.concatenate([proj[:, TILE_A], proj[:, 3 * TILE : 3 * TILE + HEAD]], axis=1)
        grad_v = jnp.concatenate([proj[:, TILE_C], proj[:, 3 * TILE + HEAD : 4 * TILE]], axis=1)
        down = summed[:1] if layer + 1 == layers else summed[at - 1 : at]
        picked += [
            before[0:1], mid[0:1], before[1:2], mid[1:2],
            grad_q.reshape(1, width), grad_v.reshape(1, width), mid[2:3], down,
        ]
        hidden_rows.append(up.reshape(1, -1))
    device = lax.axis_index("fsdp") * tp + tp_index
    last, last_hidden = norm_gain.shape[-1], up_bias.shape[-1]
    shard = lax.dynamic_slice_in_dim(jnp.concatenate(picked, axis=0), device * last, last, 1)
    shard = shard.reshape(layers, 8, last)
    hidden_shard = lax.dynamic_slice_in_dim(
        jnp.concatenate(hidden_rows, axis=0), device * last_hidden, last_hidden, 1
    )
    small_outs = [shard[:, 0:2], shard[:, 2:4], shard[:, 4:7], hidden_shard, shard[:, 7]]

    attn_sums[-1].cross([grad])
    attn_sums[-1].along(feed_sums[-1].parts)
    shards = [None] * layers
    for layer in range(layers):
        attn_shard = attn_sums[layers - 1 - layer].total()
        feed_shard = feed_sums[layers - 1 - layer].total()
        q, k, v, out = apart(attn_shard)
        shards[layer] = (q, k, v, out.T, feed_shard[:, :hidden_cols], feed_shard[:, hidden_cols:].T)
    stacked = [jnp.stack([shards[layer][n] for layer in range(layers)]) for n in range(6)]
    return (stream.astype(bf16), grad, *stacked, *small_outs)


def solution(mesh):
    tokens_spec = P(BOTH, None)
    in_spec, out_spec = P(None, "fsdp", "tp"), P(None, "tp", "fsdp")
    matrices = (in_spec, in_spec, in_spec, out_spec, in_spec, out_spec)
    smalls = (P(None, None, BOTH),) * 3 + (P(None, BOTH),) * 2
    return jax.shard_map(
        on_device,
        mesh=mesh,
        in_specs=(tokens_spec, tokens_spec, P("fsdp", None)) + matrices + smalls,
        out_specs=(tokens_spec, tokens_spec) + matrices + smalls,
        check_vma=False,
    )
```

```python
import functools

import jax
import jax.numpy as jnp
from jax import lax
from jax.experimental import pallas as pl
from jax.experimental.pallas import tpu as pltpu
from jax.sharding import PartitionSpec as P

HEAD = 64
QROWS = 256
QROWS_FORWARD = 256
eps = 1e-05
masked_fill = -1e30
VMEM_BYTES = 56 * 1024 * 1024
BOTH = ("fsdp", "tp")

f32 = jnp.float32
bf16 = jnp.bfloat16


def dot_nn(left, right):
    return lax.dot_general(left, right, (((1,), (0,)), ((), ())), preferred_element_type=f32)


def dot_nt(left, right):
    return lax.dot_general(left, right, (((1,), (1,)), ((), ())), preferred_element_type=f32)


def dot_tn(left, right):
    return lax.dot_general(left, right, (((0,), (0,)), ((), ())), preferred_element_type=f32)


def tie(value, deps):
    deps = list(deps)
    if not deps:
        return value
    return pl.pallas_call(
        lambda *refs: None,
        in_specs=[pl.BlockSpec(memory_space=pl.ANY)] * (1 + len(deps)),
        out_specs=pl.BlockSpec(memory_space=pl.ANY),
        out_shape=jax.ShapeDtypeStruct(value.shape, value.dtype),
        input_output_aliases={0: 0},
        name="tie",
    )(value, *deps)


def dep_specs(deps):
    return [pl.BlockSpec(memory_space=pl.ANY)] * len(deps)


def skip_deps(body, inputs, count):
    return lambda *refs: body(*refs[:inputs], *refs[inputs + count :])


def cost_of(products):
    return pl.CostEstimate(flops=2 * products * 512**3, bytes_accessed=1000, transcendentals=0)


COSTS = dict(
    attend_forward=16, attend_backward=26, feed_forward=9, feed_backward=14, norm_forward=3, norm_backward=6,
    stack_small=2
)


TILE = 2 * HEAD
PROJECTED = 5 * TILE
TILE_A, TILE_B, TILE_C, TILE_D, TILE_E = (slice(n * TILE, (n + 1) * TILE) for n in range(5))
FIRST, SECOND = slice(0, TILE), slice(TILE, 2 * TILE)
HEADS_OF_PART = (
    (TILE_A, TILE_B, TILE_C, 0, 0, SECOND),
    (TILE_A, TILE_B, TILE_C, 1, 1, SECOND),
    (TILE_D, TILE_E, TILE_D, 0, 1, FIRST),
)


def fill_bias(seg_q_ref, seg_k_ref, bias_ref, rows, block):
    window = rows + block
    for first in range(0, rows, block):
        row_pos = rows + first + lax.broadcasted_iota(jnp.int32, (block, window), 0)
        col_pos = first + lax.broadcasted_iota(jnp.int32, (block, window), 1)
        same = seg_q_ref[first : first + block, :] == seg_k_ref[:, first : first + window]
        bias_ref[first : first + block, :] = jnp.where(same & (col_pos <= row_pos), 0.0, masked_fill)


def fill_bias_turned(seg_q_ref, seg_k_ref, bias_ref, rows, block):
    window = rows + block
    for first in range(0, rows, block):
        row_pos = rows + first + lax.broadcasted_iota(jnp.int32, (window, block), 1)
        col_pos = first + lax.broadcasted_iota(jnp.int32, (window, block), 0)
        same = seg_q_ref[:, first : first + block] == seg_k_ref[first : first + window, :]
        bias_ref[first // block] = jnp.where(same & (col_pos <= row_pos), 0.0, masked_fill)


def halves(block):
    low = lax.broadcasted_iota(jnp.int32, (block, TILE), 1) < HEAD
    return low, ~low


def attend_forward_body(
    rows, seg_q_ref, seg_k_ref, halo_ref, own_ref, w_ref, b_ref, acc_ref, row_ref,
    p_ref, att_ref, lse_ref, out_ref, bias_ref,
):
    window = rows + QROWS_FORWARD

    @pl.when(pl.program_id(0) == 0)
    def _():
        fill_bias(seg_q_ref, seg_k_ref, bias_ref, rows, QROWS_FORWARD)
        out_ref[...] = acc_ref[...] + row_ref[...]

    weight = w_ref[0, :, :PROJECTED]
    p_ref[0, :rows] = (dot_nn(halo_ref[...], weight) + b_ref[0]).astype(bf16)
    p_ref[0, rows:] = (dot_nn(own_ref[...], weight) + b_ref[0]).astype(bf16)
    half = halves(QROWS_FORWARD)
    for first in range(0, rows, QROWS_FORWARD):
        here = slice(first, first + QROWS_FORWARD)
        own = slice(rows + first, rows + first + QROWS_FORWARD)
        span = slice(first, first + window)
        bias = bias_ref[here, :]
        outs, lses = [], []
        for q_tile, k_tile, v_tile, q_half, _, _ in HEADS_OF_PART:
            queries = jnp.where(half[q_half], p_ref[0, own, q_tile] * jnp.asarray(HEAD**-0.5, bf16), 0)
            scores = dot_nt(queries, p_ref[0, span, k_tile]) + bias
            top = jnp.max(scores, axis=-1, keepdims=True)
            terms = jnp.exp(scores - top)
            total = jnp.sum(terms, axis=-1, keepdims=True)
            outs.append(dot_nn(terms.astype(bf16), p_ref[0, span, v_tile]) * (1.0 / total))
            lses.append(top + jnp.log(total))
        att_ref[0, here, FIRST] = jnp.where(half[0], 0.0, outs[2]).astype(bf16)
        att_ref[0, here, SECOND] = jnp.where(half[0], outs[0], outs[1]).astype(bf16)
        lse_ref[0, here, FIRST] = jnp.broadcast_to(lses[2], (QROWS_FORWARD, TILE))
        lse_ref[0, here, SECOND] = jnp.where(half[0], lses[0], lses[1])
    out_ref[...] += dot_nt(att_ref[0], w_ref[0, :, 4 * TILE :])


def attend_backward_body(
    rows, first_call, seg_q_ref, seg_k_ref, g_ref, halo_ref, own_ref, w_ref, p_ref, att_ref, lse_ref,
    acc_ref, gw_ref, gb_ref, dn_ref, low_ref, bias_ref, dp_ref,
):
    window = rows + QROWS

    @pl.when(pl.program_id(0) == 0)
    def _():
        fill_bias_turned(seg_q_ref, seg_k_ref, bias_ref, rows, QROWS)
        if first_call:
            dn_ref[...] = jnp.zeros_like(dn_ref)
        else:
            dn_ref[...] = acc_ref[...]

    dp_ref[...] = jnp.zeros_like(dp_ref)
    grads = dot_nn(g_ref[...], w_ref[0, :, 4 * TILE :]).astype(bf16)
    half = halves(QROWS)
    for first in range(0, rows, QROWS):
        here = slice(first, first + QROWS)
        own = slice(rows + first, rows + first + QROWS)
        span = slice(first, first + window)
        bias = bias_ref[first // QROWS]
        lses = [lse_ref[0, here, tile].T for tile in (FIRST, SECOND)]
        products = [
            (grads[here, tile].astype(f32) * att_ref[0, here, tile].astype(f32)).T
            for tile in (FIRST, SECOND)
        ]
        dqs = []
        for head, (q_tile, k_tile, v_tile, q_half, v_half, a_tile) in enumerate(HEADS_OF_PART):
            queries = jnp.where(half[q_half], p_ref[0, own, q_tile] * jnp.asarray(HEAD**-0.5, bf16), 0)
            keys = p_ref[0, span, k_tile]
            grad = jnp.where(half[v_half], grads[here, a_tile], 0)
            which = 0 if a_tile == FIRST else 1
            lanes = slice(v_half * HEAD, v_half * HEAD + HEAD)
            inner = jnp.sum(products[which][lanes], axis=0, keepdims=True)
            lse = lses[which][v_half * HEAD : v_half * HEAD + 1]
            probs = jnp.exp(dot_nt(keys, queries) + bias - lse)
            draw = (probs * (dot_nt(p_ref[0, span, v_tile], grad) - inner)).astype(bf16)
            dp_ref[span, v_tile] += dot_nn(probs.astype(bf16), grad)
            dp_ref[span, k_tile] += dot_nn(draw, queries)
            dqs.append(dot_tn(draw, keys))
        dp_ref[own, TILE_A] = jnp.where(half[0], dqs[0], dqs[1]) * HEAD**-0.5
        dp_ref[own, TILE_D] += jnp.where(half[0], dqs[2], 0.0) * HEAD**-0.5
    dp = dp_ref[...].astype(bf16)
    gb_ref[0, :, :PROJECTED] = jnp.sum(dp.astype(f32), axis=0, keepdims=True)
    gb_ref[0, :, PROJECTED:] = jnp.zeros((1, gb_ref.shape[2] - PROJECTED), f32)
    halo_dp, own_dp = dp[:rows], dp[rows:]
    by_rows = dot_tn(halo_ref[...], halo_dp) + dot_tn(own_ref[...], own_dp)
    shared = dot_tn(g_ref[...], att_ref[0])
    gw_ref[0, :, : 4 * TILE] = by_rows[:, : 4 * TILE].astype(bf16)
    gw_ref[0, :, TILE_E] = (by_rows[:, TILE_E] + shared[:, FIRST]).astype(bf16)
    gw_ref[0, :, 5 * TILE :] = shared[:, SECOND].astype(bf16)
    dn_ref[...] += dot_nt(dp, w_ref[0, :, :PROJECTED])

    @pl.when(pl.program_id(0) == pl.num_programs(0) - 1)
    def _():
        low_ref[...] = dn_ref[:rows].astype(bf16)


def whole_spec(shape):
    return pl.BlockSpec(shape, lambda *_: (0,) * len(shape))


def part_spec(shape):
    return pl.BlockSpec((1,) + shape, lambda t: (t, 0, 0))


def call_parts(body, parts, ins, outs, scratch, name, operands, deps):
    deps = list(deps)
    in_specs = [
        part_spec(value.shape[1:]) if split else whole_spec(value.shape)
        for value, split in zip(operands, ins)
    ]
    return pl.pallas_call(
        skip_deps(body, len(operands), len(deps)),
        grid=(parts,),
        in_specs=in_specs + dep_specs(deps),
        out_specs=[part_spec(shape[1:]) if split else whole_spec(shape) for shape, _, split in outs],
        out_shape=[jax.ShapeDtypeStruct(shape, dtype) for shape, dtype, _ in outs],
        scratch_shapes=scratch,
        compiler_params=pltpu.CompilerParams(vmem_limit_bytes=VMEM_BYTES),
        cost_estimate=cost_of(COSTS[name]),
        name=name,
    )(*operands, *deps)


def attend_forward(seg_q, seg_k, halo, own, weight, bias, acc, row, deps=()):
    parts, width, _ = weight.shape
    rows = own.shape[0]
    return call_parts(
        functools.partial(attend_forward_body, rows),
        parts,
        (False, False, False, False, True, True, False, False),
        [
            ((parts, 2 * rows, PROJECTED), bf16, True),
            ((parts, rows, 2 * TILE), bf16, True),
            ((parts, rows, 2 * TILE), f32, True),
            ((rows, width), f32, False),
        ],
        [pltpu.VMEM((rows, rows + QROWS_FORWARD), f32)],
        "attend_forward",
        (seg_q, seg_k, halo, own, weight, bias, acc, row),
        deps,
    )


def attend_backward(seg_q, seg_k, grad, halo, own, weight, projected, attended, lse, acc, deps=()):
    parts, width, cols = weight.shape
    rows = grad.shape[0]
    first_call = acc is None
    return call_parts(
        functools.partial(attend_backward_body, rows, first_call),
        parts,
        (False, False, False, False, False, True, True, True, True, False),
        [
            ((parts, width, cols), bf16, True),
            ((parts, 1, cols), f32, True),
            ((2 * rows, width), f32, False),
            ((rows, width), bf16, False),
        ],
        [
            pltpu.VMEM((rows // QROWS, rows + QROWS, QROWS), f32),
            pltpu.VMEM((2 * rows, PROJECTED), f32),
        ],
        "attend_backward",
        (seg_q, seg_k, grad, halo, own, weight, projected, attended, lse, seg_q if first_call else acc),
        deps,
    )


GELU_A = 0.7978845608028654
GELU_B = 0.044715


def gelu_parts(pre):
    square = pre * pre
    bend = jnp.tanh(GELU_A * pre * (1.0 + GELU_B * square))
    half = 0.5 * (1.0 + bend)
    slope = half + 0.5 * pre * (1.0 - bend * bend) * (GELU_A * (1.0 + 3.0 * GELU_B * square))
    return pre * half, slope


def feed_forward_body(n_ref, w_ref, bias_ref, acc_ref, row_ref, pre_ref, out_ref):
    @pl.when(pl.program_id(0) == 0)
    def _():
        out_ref[...] = acc_ref[...] + row_ref[...]

    cols = pre_ref.shape[2]
    pre = dot_nn(n_ref[...], w_ref[0, :, :cols]) + bias_ref[0]
    pre_ref[0] = pre
    hidden = gelu_parts(pre)[0].astype(bf16)
    out_ref[...] += dot_nt(hidden, w_ref[0, :, cols:])


def feed_forward(normed, weight, bias, acc, row, deps=()):
    rows, width = normed.shape
    parts, _, cols = weight.shape
    return call_parts(
        feed_forward_body,
        parts,
        (False, True, True, False, False),
        [((parts, rows, cols // 2), f32, True), ((rows, width), f32, False)],
        [],
        "feed_forward",
        (normed, weight, bias, acc, row),
        deps,
    )


def feed_backward_body(first_call, g_ref, n_ref, pre_ref, w_ref, acc_ref, gw_ref, gbias_ref, dn_ref):
    @pl.when(pl.program_id(0) == 0)
    def _():
        if first_call:
            dn_ref[...] = jnp.zeros_like(dn_ref)
        else:
            dn_ref[...] = acc_ref[...]

    hidden, slope = gelu_parts(pre_ref[0])
    cols = hidden.shape[1]
    gw_ref[0, :, cols:] = dot_tn(g_ref[...], hidden.astype(bf16)).astype(bf16)
    dpre = (dot_nn(g_ref[...], w_ref[0, :, cols:]) * slope).astype(bf16)
    gbias_ref[0] = jnp.sum(dpre.astype(f32), axis=0, keepdims=True)
    gw_ref[0, :, :cols] = dot_tn(n_ref[...], dpre).astype(bf16)
    dn_ref[...] += dot_nt(dpre, w_ref[0, :, :cols])


def feed_backward(grad, normed, pre, weight, acc, deps=()):
    rows, width = normed.shape
    parts, _, cols = weight.shape
    first_call = acc is None
    return call_parts(
        functools.partial(feed_backward_body, first_call),
        parts,
        (False, False, True, True, False),
        [
            ((parts, width, cols), bf16, True),
            ((parts, 1, cols // 2), f32, True),
            ((rows, width), f32, False),
        ],
        [],
        "feed_backward",
        (grad, normed, pre, weight, normed if first_call else acc),
        deps,
    )


def norm_stats(values):
    mean = jnp.mean(values, axis=-1, keepdims=True)
    centred = values - mean
    var = jnp.mean(centred * centred, axis=-1, keepdims=True)
    scale = lax.rsqrt(var + eps)
    return centred * scale, scale


def norm_forward_body(x_ref, gain_ref, shift_ref, out_ref):
    out_ref[...] = (norm_stats(x_ref[...])[0] * gain_ref[...] + shift_ref[...]).astype(bf16)


def call_whole(body, outs, name, operands, deps=()):
    deps = list(deps)
    return pl.pallas_call(
        skip_deps(body, len(operands), len(deps)),
        in_specs=[pl.BlockSpec(memory_space=pltpu.VMEM)] * len(operands) + dep_specs(deps),
        out_specs=[pl.BlockSpec(memory_space=pltpu.VMEM)] * len(outs),
        out_shape=[jax.ShapeDtypeStruct(shape, dtype) for shape, dtype in outs],
        compiler_params=pltpu.CompilerParams(vmem_limit_bytes=VMEM_BYTES),
        cost_estimate=cost_of(COSTS[name]),
        name=name,
    )(*operands, *deps)


def norm_forward(values, gain, shift):
    return call_whole(
        norm_forward_body, [(values.shape, bf16)], "norm_forward", (values, gain[None], shift[None])
    )[0]


def norm_backward_body(x_ref, gain_ref, dn_ref, more_ref, g_ref, out_ref, low_ref, sums_ref):
    unit, scale = norm_stats(x_ref[...])
    rows = x_ref.shape[0]
    grad = dn_ref[dn_ref.shape[0] - rows :, :]
    if more_ref is not None:
        grad = grad + more_ref[...].astype(f32)
    inner = grad * gain_ref[...]
    back = scale * (
        inner
        - jnp.mean(inner, axis=-1, keepdims=True)
        - unit * jnp.mean(inner * unit, axis=-1, keepdims=True)
    )
    total = g_ref[...] + back
    out_ref[...] = total
    low_ref[...] = total.astype(bf16)
    sums_ref[0:1] = jnp.sum(grad * unit, axis=0, keepdims=True)
    sums_ref[1:2] = jnp.sum(grad, axis=0, keepdims=True)
    sums_ref[2:3] = jnp.sum(total, axis=0, keepdims=True)


def norm_backward(values, gain, dn, more, grad, deps=()):
    rows, width = values.shape
    outs = [((rows, width), f32), ((rows, width), bf16), ((3, width), f32)]
    if more is None:
        return call_whole(
            lambda x, gain, dn, *rest: norm_backward_body(x, gain, dn, None, *rest),
            outs, "norm_backward", (values, gain[None], dn, grad), deps,
        )
    return call_whole(norm_backward_body, outs, "norm_backward", (values, gain[None], dn, more, grad), deps)


def stack_small_body(core_ref, *refs):
    *row_refs, out_ref = refs
    out_ref[...] = jnp.zeros_like(out_ref)
    first = core_ref[...] == 0
    out_ref[0:1] = row_refs[0][...]
    at = 1
    for start in range(1, len(row_refs), 6):
        proj_mine, proj_other, up_mine, up_other, mid, before = row_refs[start : start + 6]
        for mine, other in ((proj_mine, proj_other), (up_mine, up_other)):
            for part in range(2):
                out_ref[at + part : at + part + 1] = jnp.where(first, mine[part], other[part])
                out_ref[at + 2 + part : at + 3 + part] = jnp.where(first, other[part], mine[part])
            at += 4
        out_ref[at : at + 3] = mid[...]
        out_ref[at + 3 : at + 6] = before[...]
        at += 6


def stack_small(core, rows):
    count = 1 + 14 * (len(rows) // 6)
    shape = (-(-count // 8) * 8, rows[0].shape[1])
    return call_whole(stack_small_body, [(shape, f32)], "stack_small", (core.reshape(1, 1), *rows))[0]


def hop(value, axis, move):
    count = lax.axis_size(axis)
    return lax.ppermute(value, axis, [(i, move(i)) for i in range(count)])


def hop_x(value):
    return hop(value, "tp", lambda i: i ^ 2)


def hop_core(value):
    return hop(value, "tp", lambda i: i ^ 1)


def hop_y(value):
    return hop(value, "fsdp", lambda i: i ^ 1)


def hop_z(value, step):
    count = lax.axis_size("fsdp")
    return hop(value, "fsdp", lambda i: (i + 2 * step) % count)


def places():
    fsdp_index, tp_index = lax.axis_index("fsdp"), lax.axis_index("tp")
    return tp_index // 2, tp_index % 2, fsdp_index // 2, fsdp_index % 2


def gather_line(shard):
    deep = lax.axis_size("fsdp") // 2
    z = places()[2]
    arrived = [hop_z(shard, step) for step in range(1, deep)]
    line = lax.dynamic_update_slice(
        jnp.zeros((deep,) + shard.shape, shard.dtype), shard[None], (z,) + (0,) * shard.ndim
    )
    for step, piece in enumerate(arrived, 1):
        line = lax.dynamic_update_slice(line, piece[None], ((z - step) % deep,) + (0,) * shard.ndim)
    return line, arrived


class Gather:
    def __init__(self, shard, after=()):
        self.line, self.parts = gather_line(tie(shard, after))

    def cross(self, after=()):
        self.line = tie(self.line, after)
        self.parts = [hop_x(self.line), hop_y(self.line)]

    def relay(self, after=()):
        half = self.line.shape[2] // 2
        self.by_x, self.by_y = (tie(part, after) for part in self.parts)
        self.parts = [hop_x(self.by_y[:, :, :half]), hop_y(self.by_x[:, :, half:])]

    def both_cores(self):
        deep, rows, cols = self.line.shape
        x, _, _, y = places()
        mine = jnp.zeros((2, deep, 2, rows, cols), self.line.dtype)
        for piece, at_x, at_y, at_col in (
            (self.line, x, y, 0),
            (self.by_x, 1 - x, y, 0),
            (self.by_y, x, 1 - y, 0),
            (self.parts[0], 1 - x, 1 - y, 0),
            (self.parts[1], 1 - x, 1 - y, cols // 2),
        ):
            mine = lax.dynamic_update_slice(mine, piece[None, :, None], (at_x, 0, at_y, 0, at_col))
        mine = mine.reshape(2, deep * 2 * rows, cols)
        return mine, hop_core(mine)


def gather_small(values):
    x, core, _, y = places()

    def both(value, index, move):
        other = move(value)
        return jnp.where(index == 0, jnp.stack([value, other]), jnp.stack([other, value]))

    whole = gather_line(both(both(both(values, core, hop_core), x, hop_x), y, hop_y))[0]
    return whole.reshape(-1, values.shape[0])


def sum_small(values):
    deep = lax.axis_size("fsdp") // 2
    for move in (hop_core, hop_x, hop_y):
        values = values + move(values)
    return sum((hop_z(values, step) for step in range(1, deep)), values)


def add_low(*values):
    return sum(value.astype(f32) for value in values).astype(bf16)


def pick(value, index, axis):
    return lax.dynamic_index_in_dim(value, index, axis, keepdims=False)


class Scatter:
    def __init__(self, other):
        self.parts = [hop_core(other)]

    def keep(self, mine):
        deep = lax.axis_size("fsdp") // 2
        x, _, _, y = places()
        cols = mine.shape[2]
        half = cols // 2
        both = [part.reshape(2, deep, 2, -1, cols) for part in (mine, self.parts[0])]
        self.left, self.right = [part[..., :half] for part in both], [part[..., half:] for part in both]
        self.sends = [
            add_low(*(pick(part, 1 - x, 0) for part in self.left)),
            add_low(*(pick(part, 1 - y, 2) for part in self.right)),
        ]
        self.parts = [hop_x(self.sends[0]), hop_y(self.sends[1])]

    def cross(self, after=()):
        x, _, _, y = places()
        by_x, by_y = (tie(part, after) for part in self.parts)
        self.left = add_low(*(pick(part, x, 0) for part in self.left), by_x)
        self.right = add_low(*(pick(part, y, 2) for part in self.right), by_y)
        self.parts = [hop_y(pick(self.left, 1 - y, 1)), hop_x(pick(self.right, 1 - x, 0))]

    def along(self, after=()):
        deep = lax.axis_size("fsdp") // 2
        x, _, z, y = places()
        by_y, by_x = (tie(part, after) for part in self.parts)
        left = add_low(pick(self.left, y, 1), by_y)
        right = add_low(pick(self.right, x, 0), by_x)
        self.line = jnp.concatenate([left, right], axis=2)
        self.parts = [
            hop_z(pick(self.line, (z + step) % deep, 0), step) for step in range(1, deep)
        ]

    def total(self, after=()):
        total = pick(self.line, places()[2], 0).astype(f32)
        for piece in (tie(part, after) for part in self.parts):
            total = total + piece.astype(f32)
        return total


def from_previous(rows):
    tp = lax.axis_size("tp")
    return lax.ppermute(rows, "tp", [(i, i + 1) for i in range(tp - 1)])


def to_previous(rows):
    tp = lax.axis_size("tp")
    return lax.ppermute(rows, "tp", [(i + 1, i) for i in range(tp - 1)])


def on_device(
    tokens, cotangent, lengths, w_query, w_key, w_value, w_out, w_up, w_down,
    norm_gain, norm_shift, attn_bias, up_bias, down_bias,
):
    fsdp, tp = lax.axis_size("fsdp"), lax.axis_size("tp")
    devices = fsdp * tp
    tp_index = lax.axis_index("tp")
    rows, width = tokens.shape
    layers = w_query.shape[0]
    head_cols, hidden_cols = w_query.shape[2], w_up.shape[2]

    def attn_columns(q, k, v, out):
        tiles = [q[:, :TILE], k[:, :TILE], v[:, :TILE], q[:, TILE:], v[:, TILE:], k[:, TILE:]]
        return jnp.concatenate(tiles + [out[:, TILE:], out[:, :TILE]], axis=1)

    def apart(value):
        at = [0, TILE, 2 * TILE, 3 * TILE, 3 * TILE + HEAD, 4 * TILE, 4 * TILE + HEAD, 5 * TILE]
        q, k, v, q2, v2, k2, out2, out = (
            value[:, start:end] for start, end in zip(at, at[1:] + [6 * TILE])
        )
        return [jnp.concatenate(two, axis=1) for two in ((q, q2), (k, k2), (v, v2), (out, out2))]

    shards = []
    for layer in range(layers):
        shards.append(attn_columns(w_query[layer], w_key[layer], w_value[layer], w_out[layer].T))
        shards.append(jnp.concatenate([w_up[layer], w_down[layer].T], axis=1))
    attn = Gather(shards[0])

    smalls = [norm_gain, norm_shift, attn_bias, up_bias, down_bias]
    packed = jnp.concatenate([part.reshape(-1) for part in smalls])
    packed_all = gather_small(packed)
    wholes, at = [], 0
    for part in smalls:
        size, lead, last = part.size, part.shape[:-1], part.shape[-1]
        piece = packed_all[:, at : at + size].reshape((devices,) + part.shape)
        wholes.append(jnp.moveaxis(piece, 0, -2).reshape(lead + (devices * last,)))
        at += size
    gain_all, shift_all, bias_attn, bias_up, bias_down = wholes

    _, core, _, _ = places()

    def core_order(values, cols):
        lead = values.shape[:-1]
        split = values.reshape(lead + (2, 2, cols))
        return jnp.stack([pick(split, core, -2), pick(split, 1 - core, -2)], axis=len(lead))

    def part_order(values, cols):
        split = values.reshape(2, 2, cols)
        split = jnp.stack([pick(split, core, 0), pick(split, 1 - core, 0)], axis=1)
        return split.reshape(-1)

    bias_q = core_order(bias_attn[:, 0], head_cols)
    bias_v = core_order(bias_attn[:, 1], head_cols)
    none = jnp.zeros(bias_q.shape[:-1] + (TILE,), f32)
    bias_proj = jnp.concatenate(
        [bias_q[..., :TILE], none, bias_v[..., :TILE], bias_q[..., TILE:], bias_v[..., TILE:], none],
        axis=-1,
    )[:, :, :, None]
    bias_hidden = core_order(bias_up, hidden_cols)[:, :, :, None]
    no_row = jnp.zeros((1, width), f32)

    seq_ends = jnp.cumsum(lengths[0])
    first_row = tp_index * rows
    key_ids = first_row - rows + jnp.arange(2 * rows, dtype=jnp.int32)
    segments = jnp.sum((key_ids[:, None] >= seq_ends[None, :]).astype(jnp.int32), axis=1)
    segments = jnp.where(key_ids >= 0, segments, -1)
    seg_q, seg_k = segments[rows:, None], segments[None, :]
    turned_q, turned_k = segments[None, rows:], segments[:, None]

    stream = tokens.astype(f32)
    saved, weights = [], []
    feed = Gather(shards[1], attn.parts)
    attn.cross()
    attn.relay()
    along = feed.parts
    feed.cross(attn.parts)
    for layer in range(layers):
        more = layer + 1 < layers
        if more:
            next_attn = Gather(shards[2 * layer + 2], along + attn.parts)
        normed = norm_forward(stream, gain_all[layer, 0], shift_all[layer, 0])
        halo = from_previous(normed)
        attn_w = attn.both_cores()
        *kept_mine, mid = attend_forward(
            seg_q, seg_k, halo, normed, attn_w[0], bias_proj[layer, 0], stream, bias_attn[layer, 2][None],
            [feed.line],
        )
        *kept_other, mid = attend_forward(
            seg_q, seg_k, halo, normed, attn_w[1], bias_proj[layer, 1], mid, no_row,
            next_attn.parts if more else (),
        )
        feed.relay([mid])
        if more:
            next_feed = Gather(shards[2 * layer + 3], next_attn.parts + [mid])
            next_attn.cross(feed.parts)
        normed_mid = norm_forward(mid, gain_all[layer, 1], shift_all[layer, 1])
        feed_w = feed.both_cores()
        pre_mine, fed = feed_forward(
            normed_mid, feed_w[0], bias_hidden[layer, 0], mid, bias_down[layer][None]
        )
        crossed = []
        if more:
            crossed, along = next_attn.parts + next_feed.parts, next_feed.parts
            next_attn.relay([fed])
            next_feed.cross(next_attn.parts)
        pre_other, fed = feed_forward(
            normed_mid, feed_w[1], bias_hidden[layer, 1], fed, no_row, crossed
        )
        saved.append((stream, halo, normed, kept_mine, kept_other, mid, normed_mid, pre_mine, pre_other))
        weights += [attn_w, feed_w]
        stream = fed
        if more:
            attn, feed = next_attn, next_feed

    grad = cotangent.astype(f32)
    grad_low = cotangent
    small_rows = [jnp.sum(grad, axis=0, keepdims=True)]
    feed_sums, attn_sums = [], []
    for layer in reversed(range(layers)):
        attn_w, feed_w = weights[2 * layer], weights[2 * layer + 1]
        stream_in, halo, normed, kept_mine, kept_other, mid, normed_mid, pre_mine, pre_other = saved[layer]
        before_feed, before_attn = (feed_sums[-1], attn_sums[-1]) if feed_sums else (None, None)
        feed_other, up_other, dn = feed_backward(
            grad_low, normed_mid, pre_other, feed_w[1], None, before_feed.parts if before_feed else ()
        )
        feed_sum = Scatter(feed_other)
        if before_attn:
            crossed = before_attn.parts
            before_attn.cross([dn])
        feed_mine, up_mine, dn = feed_backward(
            grad_low, normed_mid, pre_mine, feed_w[0], dn,
            crossed if before_feed else (),
        )
        relayed = []
        if before_attn:
            relayed = before_attn.parts
            before_attn.along([dn])
        feed_sum.keep(feed_mine)
        grad, grad_low, sums_mid = norm_backward(
            mid, gain_all[layer, 1], dn, None, grad, feed_sum.sends
        )
        attn_other, proj_other, dn, _ = attend_backward(
            turned_q, turned_k, grad_low, halo, normed, attn_w[1], *kept_other, None, relayed
        )
        attn_sum = Scatter(attn_other)
        crossed = feed_sum.parts
        feed_sum.cross([dn])
        attn_mine, proj_mine, dn, dn_halo = attend_backward(
            turned_q, turned_k, grad_low, halo, normed, attn_w[0], *kept_mine, dn,
            crossed + (before_attn.parts if before_attn else []),
        )
        relayed = feed_sum.parts
        feed_sum.along([dn])
        attn_sum.keep(attn_mine)
        grad, grad_low, sums_in = norm_backward(
            stream_in, gain_all[layer, 0], dn, to_previous(dn_halo), grad,
            attn_sum.sends + [feed_sum.line],
        )
        feed_sums.append(feed_sum)
        attn_sums.append(attn_sum)
        small_rows += [proj_mine, proj_other, up_mine, up_other, sums_mid, sums_in]

    summed = sum_small(tie(stack_small(core, small_rows), attn_sums[-1].parts))
    picked, hidden_rows = [], []
    for layer in range(layers):
        at = 1 + 14 * (layers - 1 - layer)
        by_part = summed[at : at + 8].reshape(2, 2, 2, width).swapaxes(1, 2).reshape(2, 4, width)
        proj, up = by_part[0], by_part[1]
        mid, before = summed[at + 8 : at + 11], summed[at + 11 : at + 14]
        grad_q = jnp.concatenate([proj[:, TILE_A], proj[:, 3 * TILE : 3 * TILE + HEAD]], axis=1)
        grad_v = jnp.concatenate([proj[:, TILE_C], proj[:, 3 * TILE + HEAD : 4 * TILE]], axis=1)
        down = summed[:1] if layer + 1 == layers else summed[at - 1 : at]
        picked += [
            before[0:1], mid[0:1], before[1:2], mid[1:2],
            grad_q.reshape(1, width), grad_v.reshape(1, width), mid[2:3], down,
        ]
        hidden_rows.append(up.reshape(1, -1))
    device = lax.axis_index("fsdp") * tp + tp_index
    last, last_hidden = norm_gain.shape[-1], up_bias.shape[-1]
    shard = lax.dynamic_slice_in_dim(jnp.concatenate(picked, axis=0), device * last, last, 1)
    shard = shard.reshape(layers, 8, last)
    hidden_shard = lax.dynamic_slice_in_dim(
        jnp.concatenate(hidden_rows, axis=0), device * last_hidden, last_hidden, 1
    )
    small_outs = [shard[:, 0:2], shard[:, 2:4], shard[:, 4:7], hidden_shard, shard[:, 7]]

    attn_sums[-1].cross([grad])
    attn_sums[-1].along(feed_sums[-1].parts)
    shards = [None] * layers
    for layer in range(layers):
        attn_shard = attn_sums[layers - 1 - layer].total()
        feed_shard = feed_sums[layers - 1 - layer].total()
        q, k, v, out = apart(attn_shard)
        shards[layer] = (q, k, v, out.T, feed_shard[:, :hidden_cols], feed_shard[:, hidden_cols:].T)
    stacked = [jnp.stack([shards[layer][n] for layer in range(layers)]) for n in range(6)]
    return (stream.astype(bf16), grad, *stacked, *small_outs)


def solution(mesh):
    tokens_spec = P(BOTH, None)
    in_spec, out_spec = P(None, "fsdp", "tp"), P(None, "tp", "fsdp")
    matrices = (in_spec, in_spec, in_spec, out_spec, in_spec, out_spec)
    smalls = (P(None, None, BOTH),) * 3 + (P(None, BOTH),) * 2
    return jax.shard_map(
        on_device,
        mesh=mesh,
        in_specs=(tokens_spec, tokens_spec, P("fsdp", None)) + matrices + smalls,
        out_specs=(tokens_spec, tokens_spec) + matrices + smalls,
        check_vma=False,
    )
```
